32 devices in a mesh: expert: 16 (over z, y, x), replica: 2 (over core).
Axes of the slice: x: 2, y: 2, z: 4, core: 2. Of those that a mesh axis runs over, the one named last changes fastest.
Arguments:
- tokens: bfloat16 [8192, 1024], P(('expert', 'replica')), may hold values from -6 to 6
- routes: int32 [8192, 1], P(('expert', 'replica')), may hold values from 0 to 15; in each aligned block of 256 rows (0 to 255, 256 to 511, ...) at most 32 rows name the same one
- cotangent: bfloat16 [8192, 1024], P(('expert', 'replica')), may hold values from -6 to 6
- ln_gain: bfloat16 [2, 16, 1024], P(None, 'expert'), may hold values from 0.5 to 1.5
- ln_shift: bfloat16 [2, 16, 1024], P(None, 'expert'), may hold values from -0.59765625 to 0.59765625
- w_in: bfloat16 [2, 16, 1024, 4096], P(None, 'expert', None, 'replica'), may hold values from -0.1875 to 0.1875
- b_in: bfloat16 [2, 16, 4096], P(None, 'expert'), may hold values from -0.59765625 to 0.59765625
- w_out: bfloat16 [2, 16, 4096, 1024], P(None, 'expert', 'replica'), may hold values from -0.09375 to 0.09375
- b_out: bfloat16 [2, 16, 1024], P(None, 'expert'), may hold values from -0.59765625 to 0.59765625
- centroid: bfloat16 [16, 1024], P('expert'), may hold values from -0.125 to 0.125
Outputs:
- mixed: bfloat16 [8192, 1024], P(('expert', 'replica'))
- grad_tokens: bfloat16 [8192, 1024], P(('expert', 'replica'))
- grad_w_in: float32 [2, 16, 1024, 4096], P(None, 'expert', None, 'replica')
- grad_w_out: float32 [2, 16, 4096, 1024], P(None, 'expert', 'replica')
- grad_b_in: float32 [2, 16, 4096], P(None, 'expert')
- grad_b_out: float32 [2, 16, 1024], P(None, 'expert')
- grad_gain: float32 [2, 16, 1024], P(None, 'expert')
- grad_shift: float32 [2, 16, 1024], P(None, 'expert')
- grad_centroid: float32 [16, 1024], P('expert')
- mean_gate: float32 [16], P('expert')
- load: float32 [16], P('expert')
The draws below stay inside these ranges and needn't reach their ends.
Inputs may be any that keep to these rules, and one draw needn't show every extreme that they name: `routes`: in each aligned block of 256 rows (the rows of one device) no expert is named by more than 32 rows; every expert is named by some row.
All inputs are finite; a program needn't handle non-finite values.
Results may differ from the reference program's by a relative error of at most 0.007.
Values may be sent and summed in bfloat16 or wider, within the bound.
No kernel may reach another device: no remote copies, remote signals or barrier semaphores. Data moves between devices by JAX's collectives and lax.ppermute only.
A program may use at most 256 MiB of HBM per device.

```python
import math
import jax
import jax.numpy as jnp
import numpy as np
from jax import lax

D = 1024
FF = 4096
SUBLAYERS = 2
TOK_DEV = 256
EXPERTS = 16
TOKENS = 8192
CAPACITY = 32
N_EXPERT = 16
N_REPLICA = 2


def shard_levels(stream_key, dims, cuts, least, high):
    def one(dim, shards_of):
        steps = jax.random.uniform(jax.random.fold_in(jax.random.fold_in(stream_key, 6), dim), (shards_of,), jnp.float32, least / len(cuts), high / len(cuts))
        return jnp.repeat(jnp.exp(steps), dims[dim] // shards_of).reshape((-1,) + (1,) * (len(dims) - dim - 1))

    level = one(*cuts[0])
    for cut in cuts[1:]:
        level = level * one(*cut)
    return level


def assign_block(own_key, own, number, rows, amount, top, most, slope):
    ranking = jax.random.permutation(own_key, amount)
    packed, usual = load_shares(amount, rows * top, most, slope, True), load_shares(amount, rows * top, most, slope, False)
    places = jnp.arange(amount)

    def named(lengths, turn):
        used = int((lengths > 0).sum())
        fixed = max(1, used // 4)
        shifted = fixed + (places - fixed + turn * (used - fixed)) % max(1, amount - fixed)
        return jnp.zeros((amount,), jnp.int32).at[ranking[jnp.where(places < fixed, places, shifted)]].set(jnp.asarray(lengths, jnp.int32))

    lengths = jnp.where(number % 4 == 0, named(packed, number // 4), named(usual, number - number // 4 - 1))
    mixed = jax.random.permutation(jax.random.fold_in(own, 3), amount)
    donor, sink = mixed[0:amount // 2 * 2:2], mixed[1:amount // 2 * 2:2]
    slack = jnp.minimum(lengths[donor] - 1, most - lengths[sink]) // 2
    slack = jnp.where((donor == ranking[0]) | (sink == ranking[0]) | (lengths[sink] == 0), 0, jnp.maximum(slack, 0))
    shifted = jax.random.randint(jax.random.fold_in(own, 4), (amount // 2,), 0, 1 << 20) % (slack + 1)
    lengths = lengths.at[donor].add(-shifted).at[sink].add(shifted)
    items = jnp.searchsorted(jnp.cumsum(lengths), jnp.arange(rows * top), side="right").astype(jnp.int32)
    listing = items.reshape(top, rows).T
    listing = listing[jax.random.permutation(jax.random.fold_in(own, 1), rows)]
    turn = jax.random.randint(jax.random.fold_in(own, 2), (rows, 1), 0, top)
    return jnp.take_along_axis(listing, (jnp.arange(top)[None, :] + turn) % top, axis=1)


def load_shares(amount, total, bound, slope, full):
    portions = [(1 << 20) // math.isqrt(rank ** slope) + 1 for rank in range(1, amount + 1)]
    largest = bound if full else min(bound, max(-(-total // amount), total * portions[0] // sum(portions)))
    least = 1 if total - largest >= amount - 1 else 0
    holding, surplus = [largest] + [least] * (amount - 1), total - largest - least * (amount - 1)
    while surplus > 0:
        free = [i for i in range(1, amount) if holding[i] < largest] or [i for i in range(1, amount) if holding[i] < bound]
        pool, remaining = sum([portions[i] for i in free]), surplus
        for i in free:
            extra = min(bound - holding[i], max(1, remaining * portions[i] // pool), surplus)
            holding[i] = holding[i] + extra
            surplus = surplus - extra
    return np.array(holding)


def gaussian(own_key, shape, width, bound, cuts=(), kind=jnp.bfloat16):
    level = shard_levels(own_key, shape, cuts, -0.22, 0.18) if cuts else 1.0
    result = jax.random.normal(own_key, shape, jnp.float32) * width * level
    return jnp.minimum(jnp.maximum(result, -bound), bound).astype(kind)


def setup_inputs(seed: int = 0) -> dict:
    key_of = jax.random.split(jax.random.key(seed), 11)
    tokens = gaussian(key_of[0], (TOKENS, D), 1.0, 6.0, ((0, 32),))
    routes_keys = jax.random.split(jax.random.fold_in(key_of[1], 1), TOKENS // TOK_DEV)
    routes_turns = jax.random.permutation(jax.random.fold_in(key_of[1], 3), TOKENS // TOK_DEV)
    routes = jax.vmap(lambda own, number: assign_block(jax.random.fold_in(key_of[1], 2), own, number, TOK_DEV, EXPERTS, 1, CAPACITY, 2))(routes_keys, routes_turns).reshape((TOKENS, 1))
    cotangent = gaussian(key_of[2], (TOKENS, D), 1.0, 6.0, ((0, 32),))
    ln_gain = jnp.clip(1.0 + 0.1 * jax.random.normal(key_of[3], (SUBLAYERS, EXPERTS, D), jnp.float32), 0.5, 1.5).astype(jnp.bfloat16)
    ln_shift = gaussian(key_of[4], (SUBLAYERS, EXPERTS, D), 0.1, 0.59765625, ((1, 16),))
    w_in = gaussian(key_of[5], (SUBLAYERS, EXPERTS, D, FF), D ** -0.5, 0.1875, ((1, 16), (3, 2)))
    b_in = gaussian(key_of[6], (SUBLAYERS, EXPERTS, FF), 0.1, 0.59765625, ((1, 16),))
    w_out = gaussian(key_of[7], (SUBLAYERS, EXPERTS, FF, D), FF ** -0.5, 0.09375, ((1, 16), (2, 2)))
    b_out = gaussian(key_of[8], (SUBLAYERS, EXPERTS, D), 0.1, 0.59765625, ((1, 16),))
    centroid = gaussian(key_of[9], (EXPERTS, D), (2 * D) ** -0.5, 0.125, ((0, 16),))
    return {"tokens": tokens, "routes": routes, "cotangent": cotangent, "ln_gain": ln_gain, "ln_shift": ln_shift, "w_in": w_in, "b_in": b_in, "w_out": w_out, "b_out": b_out, "centroid": centroid}


epsilon = 1e-05
highest = lax.Precision.HIGHEST

@jax.custom_vjp
def low(v):
    return lax.optimization_barrier(v.astype(jnp.bfloat16)).astype(jnp.float32)

@jax.custom_vjp
def low_back(v):
    return v

def low_keep(v):
    return (low(v), None)

def low_pass(kept, grad):
    return (grad,)

def back_keep(v):
    return (v, None)

def back_low(kept, grad):
    return (low(grad),)
low.defvjp(low_keep, low_pass)
low_back.defvjp(back_keep, back_low)

def expert_branch(picked, valid, gain, shift, w_first, b_first, w_second, b_second, center):
    inputs = low_back(picked)
    logits = jnp.dot(inputs, center, precision=highest)
    gate_value = jax.nn.sigmoid(logits)
    state = inputs
    for layer in range(SUBLAYERS):
        average = lax.optimization_barrier(jnp.mean(state, axis=1, keepdims=True))
        centered = state - average
        variance = lax.optimization_barrier(jnp.mean(centered * centered, axis=1, keepdims=True))
        normed = centered * lax.rsqrt(variance + epsilon)
        lowered = low(normed * gain[layer] + shift[layer])
        hidden = low_back(jnp.dot(lowered, w_first[layer], precision=highest) + b_first[layer])
        activated = low(jax.nn.gelu(hidden, approximate=False))
        second = low_back(jnp.dot(activated, w_second[layer], precision=highest) + b_second[layer])
        state = state + second
    branch = low(gate_value[:, None] * state)
    return jnp.where(valid[:, None], branch, jnp.zeros_like(branch))

def reference(tokens, routes, cotangent, ln_gain, ln_shift, w_in, b_in, w_out, b_out, centroid):
    route = routes[:, 0].astype(jnp.int32)
    labels = jnp.arange(EXPERTS, dtype=jnp.int32)
    onehot = route[:, None] == labels[None, :]
    counts = lax.optimization_barrier(jnp.sum(onehot.astype(jnp.int32), axis=0))
    starts = jnp.cumsum(counts) - counts
    ordered = jnp.argsort(route, stable=True).astype(jnp.int32)
    padded = CAPACITY * N_EXPERT * N_REPLICA
    places = jnp.arange(padded, dtype=jnp.int32)
    valid = places[None, :] < counts[:, None]
    where_at = jnp.minimum(starts[:, None] + places[None, :], TOKENS - 1).astype(jnp.int32)
    picks = jnp.take(ordered, where_at, axis=0).astype(jnp.int32)

    def forward(inputs, gain, shift, w_first, b_first, w_second, b_second, center):

        def one_expert(member):
            picked = jnp.take(inputs, member[0], axis=0)
            return expert_branch(picked, member[1], member[2], member[3], member[4], member[5], member[6], member[7], member[8])
        members = (picks, valid, jnp.swapaxes(gain, 0, 1), jnp.swapaxes(shift, 0, 1), jnp.swapaxes(w_first, 0, 1), jnp.swapaxes(b_first, 0, 1), jnp.swapaxes(w_second, 0, 1), jnp.swapaxes(b_second, 0, 1), center)
        stacked = lax.map(jax.checkpoint(one_expert), members)
        total = jnp.zeros_like(inputs).at[picks.reshape(-1)].add(stacked.reshape(-1, D))
        return inputs + total
    values = (tokens.astype(jnp.float32), ln_gain.astype(jnp.float32), ln_shift.astype(jnp.float32), w_in.astype(jnp.float32), b_in.astype(jnp.float32), w_out.astype(jnp.float32), b_out.astype(jnp.float32), centroid.astype(jnp.float32))
    mixed_full, pullback = jax.vjp(forward, *values)
    grads = pullback(cotangent.astype(jnp.float32))
    inputs = values[0]
    chosen = jnp.take(values[7], route, axis=0)
    gate_token = jax.nn.sigmoid(lax.optimization_barrier(jnp.sum(inputs * chosen, axis=1)))
    gate_sum = lax.optimization_barrier(jnp.sum(jnp.where(onehot, gate_token[:, None], jnp.zeros_like(gate_token)[:, None]), axis=0))
    counted = counts.astype(jnp.float32)
    mean_gate = gate_sum / counted
    load = counted * EXPERTS / TOKENS
    return (mixed_full.astype(jnp.bfloat16), grads[0].astype(jnp.bfloat16), grads[3], grads[5], grads[4], grads[6], grads[1], grads[2], grads[7], mean_gate, load)
```

```python
import jax
import jax.numpy as jnp
from jax import lax
from jax.experimental import pallas as pl
from jax.experimental.pallas import tpu as pltpu
from jax.sharding import PartitionSpec as P

EPS = 1e-05
F32 = jnp.float32
BF16 = jnp.bfloat16
PAD_MARK = 64.0
PAD_LIMIT = 32.0
SWAP = [(0, 1), (1, 0)]


def dot_nn(a, b):
    return lax.dot_general(a, b, (((1,), (0,)), ((), ())), preferred_element_type=F32)


def dot_nt(a, b):
    return lax.dot_general(a, b, (((1,), (1,)), ((), ())), preferred_element_type=F32)


def dot_tn(a, b):
    return lax.dot_general(a, b, (((0,), (0,)), ((), ())), preferred_element_type=F32)


def gelu_and_slope(v):
    e = jnp.exp(v * v * -0.5)
    t = 1.0 / (1.0 + 0.23164189 * jnp.abs(v))
    q = t * (0.127414796 + t * (-0.142248368 + t * (0.7107068705 + t * (-0.7265760135 + t * 0.5307027145))))
    q = q * e
    phi = jnp.where(v >= 0.0, 1.0 - q, q)
    return v * phi, phi + v * (e * 0.3989422804014327)


def params(mib=56):
    return pltpu.CompilerParams(vmem_limit_bytes=mib << 20)


def cost():
    return pl.CostEstimate(flops=0, bytes_accessed=0, transcendentals=0)


def whole(shape):
    return pl.BlockSpec(shape, lambda *_: (0,) * len(shape))


def sds(shape, dtype):
    return jax.ShapeDtypeStruct(shape, dtype)


def slots_kernel(experts, capacity, routes_ref, slot_ref):
    n = routes_ref.shape[0]
    lanes = max(128, experts)
    route = routes_ref[...]
    onehot = route == lax.broadcasted_iota(jnp.int32, (n, lanes), 1)
    hot = jnp.where(onehot, 1.0, 0.0)
    rows = lax.broadcasted_iota(jnp.int32, (n, n), 0)
    cols = lax.broadcasted_iota(jnp.int32, (n, n), 1)
    lower = jnp.where(cols < rows, 1.0, 0.0).astype(BF16)
    earlier = dot_nn(lower, hot.astype(BF16))
    rank = jnp.sum(earlier * hot, axis=1, keepdims=True)
    slot_ref[...] = route * capacity + rank.astype(jnp.int32)


def spread(slot, slots):
    n = slot.shape[0]
    return jnp.where(slot == lax.broadcasted_iota(jnp.int32, (n, slots), 1), 1.0, 0.0)


def pack_kernel(marked, slot_ref, values_ref, out_ref):
    slots = out_ref.shape[0]
    hot = spread(slot_ref[...], slots).astype(BF16)
    packed = dot_tn(hot, values_ref[...])
    out_ref[...] = packed.astype(BF16)
    if marked:
        filled = dot_tn(hot, jnp.ones((hot.shape[0], 128), BF16))
        first = packed[:, :128] + (1.0 - filled) * PAD_MARK
        out_ref[:, :128] = first.astype(BF16)


def pack(marked, slot, values, slots):
    return pl.pallas_call(
        lambda *refs: pack_kernel(marked, *refs),
        out_shape=sds((slots, values.shape[1]), BF16),
        compiler_params=params(),
        cost_estimate=cost(),
        name="pack",
    )(slot, values)


def unpack_kernel(slot_ref, returned_ref, base_ref, out_ref):
    hot = spread(slot_ref[...], returned_ref.shape[0]).astype(BF16)
    picked = dot_nn(hot, returned_ref[...])
    out_ref[...] = (base_ref[...].astype(F32) + picked).astype(BF16)


def unpack(slot, returned, base):
    return pl.pallas_call(
        unpack_kernel,
        out_shape=sds(base.shape, BF16),
        compiler_params=params(),
        cost_estimate=cost(),
        name="unpack",
    )(slot, returned, base)


def norm_stats(h):
    mu = jnp.mean(h, axis=1, keepdims=True)
    c = h - mu
    r = lax.rsqrt(jnp.mean(c * c, axis=1, keepdims=True) + EPS)
    return mu, r, c * r


def ffn_step(low_ref, w_in_ref, b_in_ref, w_out_ref, act_ref, slope_ref, acc_ref):
    hidden = dot_nn(low_ref[...], w_in_ref[...]) + b_in_ref[...].astype(F32)
    act, slope = gelu_and_slope(hidden)
    act = act.astype(BF16)
    act_ref[...] = act
    slope_ref[...] = slope.astype(BF16)
    acc_ref[...] += dot_nn(act, w_out_ref[...])


def first_kernel(
    x_ref, gain_ref, shift_ref, center_ref, w_in_ref, b_in_ref, w_out_ref,
    low_ref, act_ref, slope_ref, part_ref, row_ref, acc_ref,
):
    i = pl.program_id(0)

    @pl.when(i == 0)
    def _():
        x = x_ref[...].astype(F32)
        mu, r, xhat = norm_stats(x)
        low_ref[...] = (xhat * gain_ref[...].astype(F32) + shift_ref[...].astype(F32)).astype(BF16)
        logit = jnp.sum(x * center_ref[...].astype(F32), axis=1, keepdims=True)
        gate = jax.nn.sigmoid(logit)
        live = jnp.where(x[:, :1] < PAD_LIMIT, 1.0, 0.0)
        lane = lax.broadcasted_iota(jnp.int32, row_ref.shape, 1)
        row_ref[...] = jnp.where(
            lane == 0, mu, jnp.where(lane == 1, r, jnp.where(lane == 2, gate, live))
        )
        acc_ref[...] = jnp.zeros_like(acc_ref)

    ffn_step(low_ref, w_in_ref, b_in_ref, w_out_ref, act_ref, slope_ref, acc_ref)

    @pl.when(i == pl.num_programs(0) - 1)
    def _():
        part_ref[...] = acc_ref[...].astype(BF16)


def second_kernel(
    own, x_ref, mine_ref, theirs_ref, bias_ref, gain_ref, shift_ref, last_bias_ref, w_in_ref, b_in_ref, w_out_ref,
    low_ref, act_ref, slope_ref, part_ref, xhat_ref, row_ref, acc_ref,
):
    i = pl.program_id(0)

    @pl.when(i == 0)
    def _():
        h = (
            x_ref[...].astype(F32)
            + bias_ref[...].astype(F32)
            + (mine_ref[...].astype(F32) + theirs_ref[...].astype(F32))
        )
        mu, r, xhat = norm_stats(h)
        low_ref[...] = (xhat * gain_ref[...].astype(F32) + shift_ref[...].astype(F32)).astype(BF16)
        xhat_ref[...] = xhat.astype(BF16)
        row_ref[...] = jnp.broadcast_to(r, row_ref.shape)
        if own:
            acc_ref[...] = h + last_bias_ref[...].astype(F32)
        else:
            acc_ref[...] = jnp.zeros_like(acc_ref)

    ffn_step(low_ref, w_in_ref, b_in_ref, w_out_ref, act_ref, slope_ref, acc_ref)

    @pl.when(i == pl.num_programs(0) - 1)
    def _():
        part_ref[...] = acc_ref[...].astype(part_ref.dtype)


def weight_specs(layer, depth, width, blk):
    w_in = pl.BlockSpec((None, None, depth, blk), lambda i: (layer, 0, 0, i))
    b_in = pl.BlockSpec((None, 1, blk), lambda i: (layer, 0, i))
    w_out = pl.BlockSpec((None, None, blk, depth), lambda i: (layer, 0, i, 0))
    return w_in, b_in, w_out


def vec_spec(layer, depth):
    return pl.BlockSpec((None, 1, depth), lambda i: (layer, 0, 0))


def forward_first(x, gain, shift, center, w_in, b_in, w_out, blk):
    rows, depth = x.shape
    half = w_in.shape[3]
    wi, bi, wo = weight_specs(0, depth, half, blk)
    return pl.pallas_call(
        first_kernel,
        grid=(half // blk,),
        in_specs=[whole(x.shape), vec_spec(0, depth), vec_spec(0, depth), whole(center.shape), wi, bi, wo],
        out_specs=[
            whole(x.shape),
            pl.BlockSpec((rows, blk), lambda i: (0, i)),
            pl.BlockSpec((rows, blk), lambda i: (0, i)),
            whole(x.shape),
            whole((rows, 128)),
        ],
        out_shape=[
            sds(x.shape, BF16),
            sds((rows, half), BF16),
            sds((rows, half), BF16),
            sds(x.shape, BF16),
            sds((rows, 128), F32),
        ],
        scratch_shapes=[pltpu.VMEM(x.shape, F32)],
        compiler_params=params(),
        cost_estimate=cost(),
        name="forward_first",
    )(x, gain, shift, center, w_in, b_in, w_out)


def forward_second(own, x, mine, theirs, bias, gain, shift, w_in, b_in, w_out, blk):
    rows, depth = x.shape
    half = w_in.shape[3]
    wi, bi, wo = weight_specs(1, depth, half, blk)
    return pl.pallas_call(
        lambda *refs: second_kernel(own, *refs),
        grid=(half // blk,),
        in_specs=[
            whole(x.shape), whole(x.shape), whole(x.shape),
            vec_spec(0, depth), vec_spec(1, depth), vec_spec(1, depth), vec_spec(1, depth), wi, bi, wo,
        ],
        out_specs=[
            whole(x.shape),
            pl.BlockSpec((rows, blk), lambda i: (0, i)),
            pl.BlockSpec((rows, blk), lambda i: (0, i)),
            whole(x.shape),
            whole(x.shape),
            whole((rows, 128)),
        ],
        out_shape=[
            sds(x.shape, BF16),
            sds((rows, half), BF16),
            sds((rows, half), BF16),
            sds(x.shape, F32 if own else BF16),
            sds(x.shape, BF16),
            sds((rows, 128), F32),
        ],
        scratch_shapes=[pltpu.VMEM(x.shape, F32)],
        compiler_params=params(),
        cost_estimate=cost(),
        name="forward_second",
    )(x, mine, theirs, bias, gain, shift, bias, w_in, b_in, w_out)


def branch_kernel(part_ref, theirs_ref, row_ref, out_ref, branch_ref):
    out = part_ref[...] + theirs_ref[...].astype(F32)
    out_ref[...] = out
    branch_ref[...] = (row_ref[:, 2:3] * out).astype(BF16)


def gated(part, theirs, row):
    return pl.pallas_call(
        branch_kernel,
        out_shape=[sds(part.shape, F32), sds(part.shape, BF16)],
        compiler_params=params(),
        cost_estimate=cost(),
        name="gated",
    )(part, theirs, row)


def back_step(ds_ref, w_in_ref, w_out_ref, slope_ref, dh_ref, bias_ref, acc_ref):
    dact = dot_nt(ds_ref[...], w_out_ref[...])
    dh = (dact * slope_ref[...].astype(F32)).astype(BF16)
    dh_ref[...] = dh
    bias_ref[...] = jnp.sum(dh.astype(F32), axis=0, keepdims=True)
    acc_ref[...] += dot_nt(dh, w_in_ref[...])


def row_sum(v):
    return jnp.sum(v, axis=0, keepdims=True)


def back_second_kernel(
    dy_ref, row_ref, xhat_ref, w_in_ref, w_out_ref, slope_ref,
    ds_ref, dh_ref, part_ref, sums_ref, bias_ref, acc_ref,
):
    i = pl.program_id(0)

    @pl.when(i == 0)
    def _():
        ds_ref[...] = (row_ref[:, 2:3] * dy_ref[...].astype(F32)).astype(BF16)
        acc_ref[...] = jnp.zeros_like(acc_ref)

    back_step(ds_ref, w_in_ref, w_out_ref, slope_ref, dh_ref, bias_ref, acc_ref)

    @pl.when(i == pl.num_programs(0) - 1)
    def _():
        dn = acc_ref[...]
        part_ref[...] = dn.astype(BF16)
        sums_ref[0:1, :] = row_sum(dn * xhat_ref[...].astype(F32))
        sums_ref[1:2, :] = row_sum(dn)
        sums_ref[2:3, :] = row_sum(ds_ref[...].astype(F32))


def back_first_kernel(
    own, dy_ref, row_ref, mine_ref, theirs_ref, xhat_ref, row1_ref, gain_ref, x_ref, w_in_ref, w_out_ref, slope_ref,
    ds_ref, dh_ref, part_ref, sums_ref, bias_ref, *more,
):
    acc_ref = more[-1]
    i = pl.program_id(0)

    @pl.when(i == 0)
    def _():
        dn = mine_ref[...].astype(F32) + theirs_ref[...].astype(F32)
        dxhat = dn * gain_ref[...].astype(F32)
        xhat = xhat_ref[...].astype(F32)
        m1 = jnp.mean(dxhat, axis=1, keepdims=True)
        m2 = jnp.mean(dxhat * xhat, axis=1, keepdims=True)
        carry = row_ref[:, 2:3] * dy_ref[...].astype(F32) + row1_ref[:, 0:1] * (dxhat - m1 - xhat * m2)
        if own:
            more[0][...] = carry
        ds_ref[...] = carry.astype(BF16)
        acc_ref[...] = jnp.zeros_like(acc_ref)

    back_step(ds_ref, w_in_ref, w_out_ref, slope_ref, dh_ref, bias_ref, acc_ref)

    @pl.when(i == pl.num_programs(0) - 1)
    def _():
        dn = acc_ref[...]
        part_ref[...] = dn.astype(part_ref.dtype)
        xhat = (x_ref[...].astype(F32) - row_ref[:, 0:1]) * row_ref[:, 1:2]
        sums_ref[0:1, :] = row_sum(dn * xhat)
        sums_ref[1:2, :] = row_sum(dn)
        sums_ref[2:3, :] = row_sum(ds_ref[...].astype(F32))


def backward_second(dy, row, xhat, w_in, w_out, slope, blk):
    rows, depth = dy.shape
    half = w_in.shape[3]
    wi, _, wo = weight_specs(1, depth, half, blk)
    by_column = pl.BlockSpec((rows, blk), lambda i: (0, i))
    return pl.pallas_call(
        back_second_kernel,
        grid=(half // blk,),
        in_specs=[whole(dy.shape), whole(row.shape), whole(dy.shape), wi, wo, by_column],
        out_specs=[whole(dy.shape), by_column, whole(dy.shape), whole((8, depth)), pl.BlockSpec((1, blk), lambda i: (0, i))],
        out_shape=[
            sds(dy.shape, BF16),
            sds((rows, half), BF16),
            sds(dy.shape, BF16),
            sds((8, depth), F32),
            sds((1, half), F32),
        ],
        scratch_shapes=[pltpu.VMEM(dy.shape, F32)],
        compiler_params=params(),
        cost_estimate=cost(),
        name="backward_second",
    )(dy, row, xhat, w_in, w_out, slope)


def backward_first(own, dy, row, mine, theirs, xhat, row1, gain, x, w_in, w_out, slope, blk):
    rows, depth = dy.shape
    half = w_in.shape[3]
    wi, _, wo = weight_specs(0, depth, half, blk)
    by_column = pl.BlockSpec((rows, blk), lambda i: (0, i))
    full = whole(dy.shape)
    return pl.pallas_call(
        lambda *refs: back_first_kernel(own, *refs),
        grid=(half // blk,),
        in_specs=[full, whole(row.shape), full, full, full, whole(row.shape), vec_spec(1, depth), full, wi, wo, by_column],
        out_specs=[full, by_column, full, whole((8, depth)), pl.BlockSpec((1, blk), lambda i: (0, i))]
        + ([full] if own else []),
        out_shape=[
            sds(dy.shape, BF16),
            sds((rows, half), BF16),
            sds(dy.shape, F32 if own else BF16),
            sds((8, depth), F32),
            sds((1, half), F32),
        ]
        + ([sds(dy.shape, F32)] if own else []),
        scratch_shapes=[pltpu.VMEM(dy.shape, F32)],
        compiler_params=params(),
        cost_estimate=cost(),
        name="backward_first",
    )(dy, row, mine, theirs, xhat, row1, gain, x, w_in, w_out, slope)


def input_kernel(dy_ref, out_ref, row_ref, x_ref, part_ref, theirs_ref, carry_ref, gain_ref, center_ref, drow_ref, sums_ref):
    x = x_ref[...].astype(F32)
    gate = row_ref[:, 2:3]
    live = row_ref[:, 3:4]
    dgate = jnp.sum(dy_ref[...].astype(F32) * out_ref[...], axis=1, keepdims=True)
    dlogit = dgate * gate * (1.0 - gate)
    dxhat = (part_ref[...] + theirs_ref[...].astype(F32)) * gain_ref[...].astype(F32)
    r = row_ref[:, 1:2]
    xhat = (x - row_ref[:, 0:1]) * r
    m1 = jnp.mean(dxhat, axis=1, keepdims=True)
    m2 = jnp.mean(dxhat * xhat, axis=1, keepdims=True)
    carry = carry_ref[...] + r * (dxhat - m1 - xhat * m2)
    drow_ref[...] = (carry + dlogit * center_ref[...].astype(F32)).astype(BF16)
    sums_ref[0:1, :] = row_sum(dlogit * x)
    sums_ref[1:2, :] = jnp.broadcast_to(row_sum(gate * live), (1, x.shape[1]))
    sums_ref[2:3, :] = jnp.broadcast_to(row_sum(live), (1, x.shape[1]))


def input_gradient(dy, out, row, x, part, theirs, carry, gain, center):
    depth = x.shape[1]
    return pl.pallas_call(
        input_kernel,
        grid=(1,),
        in_specs=[whole(dy.shape), whole(dy.shape), whole(row.shape)] + [whole(dy.shape)] * 4
        + [vec_spec(0, depth), whole(center.shape)],
        out_specs=[whole(dy.shape), whole((8, depth))],
        out_shape=[sds(dy.shape, BF16), sds((8, depth), F32)],
        compiler_params=params(),
        cost_estimate=cost(),
        name="input_gradient",
    )(dy, out, row, x, part, theirs, carry, gain, center)


def weight_kernel(a00_ref, a01_ref, b00_ref, b01_ref, a10_ref, a11_ref, b10_ref, b11_ref, out_ref):
    layer = pl.program_id(0)

    @pl.when(layer == 0)
    def _():
        out_ref[...] = dot_tn(a00_ref[...], b00_ref[...]) + dot_tn(a01_ref[...], b01_ref[...])

    @pl.when(layer == 1)
    def _():
        out_ref[...] = dot_tn(a10_ref[...], b10_ref[...]) + dot_tn(a11_ref[...], b11_ref[...])


def weight_gradient(layers, blk):
    rows, left = layers[0][0][0].shape
    right = layers[0][1][0].shape[1]
    steps = left // blk
    last = steps - 1
    in0_a = pl.BlockSpec((rows, blk), lambda k, i: (0, jnp.where(k == 0, i, last)))
    in1_a = pl.BlockSpec((rows, blk), lambda k, i: (0, jnp.where(k == 1, i, 0)))
    b = whole((rows, right))
    args = [*layers[0][0], *layers[0][1], *layers[1][0], *layers[1][1]]
    return pl.pallas_call(
        weight_kernel,
        grid=(2, steps),
        in_specs=[in0_a, in0_a, b, b, in1_a, in1_a, b, b],
        out_specs=pl.BlockSpec((None, None, blk, right), lambda k, i: (k, 0, i, 0)),
        out_shape=sds((2, 1, left, right), F32),
        compiler_params=params(),
        cost_estimate=cost(),
        name="weight_gradient",
    )(*args)


def on_device(tokens, routes, cotangent, ln_gain, ln_shift, w_in, b_in, w_out, b_out, centroid):
    experts = lax.axis_size("expert")
    replicas = lax.axis_size("replica")
    here = lax.axis_index("replica")
    tok_dev, depth = tokens.shape
    half = w_in.shape[3]
    capacity = 2 * tok_dev // experts
    slots = experts * capacity
    blk = 512

    def exchange(v):
        moved = lax.all_to_all(
            v.reshape(experts, capacity, depth), "expert", split_axis=0, concat_axis=0, tiled=True
        )
        return moved.reshape(slots, depth)

    def swap(v):
        return lax.ppermute(v, "replica", SWAP)

    slot = pl.pallas_call(
        lambda *refs: slots_kernel(experts, capacity, *refs),
        out_shape=sds((tok_dev, 1), jnp.int32),
        compiler_params=params(),
        cost_estimate=cost(),
        name="slots",
    )(routes)
    b_half = lax.dynamic_slice_in_dim(b_in, here * half, half, axis=2)
    x_own = exchange(pack(True, slot, tokens, slots))
    x_par = swap(x_own)
    sent_cot = pack(False, slot, cotangent, slots)
    sent_cot, x_own = lax.optimization_barrier((sent_cot, x_own))
    dy_own = exchange(sent_cot)

    def first(x):
        return forward_first(x, ln_gain, ln_shift, centroid, w_in, b_half, w_out, blk)

    low0_own, act0_own, slope0_own, p0_own, row_own = first(x_own)
    p0_own_there = swap(p0_own)
    low0_par, act0_par, slope0_par, p0_par, row_par = first(x_par)
    p0_par_there = swap(p0_par)

    def second(own, x, mine, theirs):
        return forward_second(own, x, mine, theirs, b_out, ln_gain, ln_shift, w_in, b_half, w_out, blk)

    low1_par, act1_par, slope1_par, p1_par, xhat1_par, row1_par = second(False, x_par, p0_par, p0_own_there)
    p1_there = swap(p1_par)
    low1_own, act1_own, slope1_own, p1_own, xhat1_own, row1_own = second(True, x_own, p0_own, p0_par_there)
    out, branch = gated(p1_own, p1_there, row_own)
    branch, dy_own = lax.optimization_barrier((branch, dy_own))
    returned = exchange(branch)
    dy_par = swap(dy_own)

    ds1_own, dh1_own, n1_own, sums1_own, bias1_own = backward_second(
        dy_own, row_own, xhat1_own, w_in, w_out, slope1_own, blk
    )
    n1_own_there = swap(n1_own)
    ds1_par, dh1_par, n1_par, sums1_par, bias1_par = backward_second(
        dy_par, row_par, xhat1_par, w_in, w_out, slope1_par, blk
    )
    n1_par_there = swap(n1_par)
    ds0_par, dh0_par, n0_par, sums0_par, bias0_par = backward_first(
        False, dy_par, row_par, n1_par, n1_own_there, xhat1_par, row1_par, ln_gain, x_par, w_in, w_out, slope0_par, blk
    )
    n0_there = swap(n0_par)
    ds0_own, dh0_own, n0_own, sums0_own, bias0_own, carry_own = backward_first(
        True, dy_own, row_own, n1_own, n1_par_there, xhat1_own, row1_own, ln_gain, x_own, w_in, w_out, slope0_own, blk
    )
    drow, sums_in = input_gradient(
        dy_own, out, row_own, x_own, n0_own, n0_there, carry_own, ln_gain, centroid
    )
    drow, returned = lax.optimization_barrier((drow, returned))
    grad_returned = exchange(drow)

    grad_out = weight_gradient(
        [((act0_own, act0_par), (ds0_own, ds0_par)), ((act1_own, act1_par), (ds1_own, ds1_par))], 512
    )
    grad_in = weight_gradient(
        [((low0_own, low0_par), (dh0_own, dh0_par)), ((low1_own, low1_par), (dh1_own, dh1_par))], 256
    )
    mixed = unpack(slot, returned, tokens)

    sums0 = sums0_own + sums0_par
    sums1 = sums1_own + sums1_par
    bias = jnp.concatenate([bias0_own + bias0_par, bias1_own + bias1_par])
    local = jnp.concatenate([sums0, sums1, sums_in, bias.reshape(-1, depth)], axis=0)
    other = swap(local)
    total = local + other
    others_bias = other[24:].reshape(2, half)
    grad_b_in = jnp.where(
        here == 0,
        jnp.concatenate([bias, others_bias], axis=1),
        jnp.concatenate([others_bias, bias], axis=1),
    )
    grad_b_out = jnp.stack([sums0[2], sums1[2]])
    grad_gain = jnp.stack([total[0], total[8]])
    grad_shift = jnp.stack([total[1], total[9]])
    gate_total = total[17, :1]
    count_total = total[18, :1]
    grad_tokens = unpack(slot, grad_returned, cotangent)
    return (
        mixed,
        grad_tokens,
        grad_in,
        grad_out,
        grad_b_in[:, None],
        grad_b_out[:, None],
        grad_gain[:, None],
        grad_shift[:, None],
        total[16][None],
        gate_total / count_total,
        count_total / (tok_dev * replicas),
    )


def solution(mesh):
    rows = P(("expert", "replica"), None)
    by_expert = P(None, "expert", None)
    first_weight = P(None, "expert", None, "replica")
    second_weight = P(None, "expert", "replica", None)
    return jax.shard_map(
        on_device,
        mesh=mesh,
        in_specs=(
            rows, rows, rows, by_expert, by_expert, first_weight, by_expert, second_weight, by_expert,
            P("expert", None),
        ),
        out_specs=(
            rows, rows, first_weight, second_weight, by_expert, by_expert, by_expert, by_expert,
            P("expert", None), P("expert"), P("expert"),
        ),
        check_vma=False,
    )
```

```python
import jax
import jax.numpy as jnp
from jax import lax
from jax.experimental import pallas as pl
from jax.experimental.pallas import tpu as pltpu
from jax.sharding import PartitionSpec as P

EPS = 1e-05
F32 = jnp.float32
BF16 = jnp.bfloat16
PAD_MARK = 64.0
PAD_LIMIT = 32.0
SWAP = [(0, 1), (1, 0)]
VMEM = pl.BlockSpec(memory_space=pltpu.VMEM)
SMEM = pl.BlockSpec(memory_space=pltpu.SMEM)


def dot_nn(a, b):
    return lax.dot_general(a, b, (((1,), (0,)), ((), ())), preferred_element_type=F32)


def dot_nt(a, b):
    return lax.dot_general(a, b, (((1,), (1,)), ((), ())), preferred_element_type=F32)


def dot_tn(a, b):
    return lax.dot_general(a, b, (((0,), (0,)), ((), ())), preferred_element_type=F32)


def gelu_and_slope(v):
    phi = 0.5 + 0.5 * lax.erf(v * 0.7071067811865476)
    return v * phi, phi + v * (jnp.exp(v * v * -0.5) * 0.3989422804014327)


def sds(shape, dtype):
    return jax.ShapeDtypeStruct(shape, dtype)


def large(a):
    return len(a.shape) > 1 and a.shape[0] * a.shape[1] >= 1 << 16


def to_hbm(a):
    return pltpu.with_memory_space_constraint(a, pltpu.HBM) if large(a) else a


def in_hbm(o):
    return pltpu.HBM(o.shape, o.dtype) if large(o) else o


def cost():
    return pl.CostEstimate(flops=0, bytes_accessed=0, transcendentals=0)


def params(mib=52):
    return pltpu.CompilerParams(vmem_limit_bytes=mib << 20)


def call(kernel, name, args, outs, smem_in=0):
    return pl.pallas_call(
        kernel,
        in_specs=[SMEM] * smem_in + [VMEM] * (len(args) - smem_in),
        out_specs=[VMEM] * len(outs),
        out_shape=outs,
        compiler_params=params(),
        cost_estimate=cost(),
        name=name,
    )(*args)


def row_call(kernel, name, rows, args, outs, sums=0, weights=(), far=(), scratch=(), tile=256):
    steps = rows // tile
    half = steps // 2
    first = {
        "r": lambda i: i,
        "o": lambda i: jnp.minimum(i, half - 1),
        "p": lambda i: jnp.maximum(i - half, 0),
        "s": lambda i: lax.rem(i + half, steps),
    }

    def spec(kind, shape):
        if kind == "w":
            return pl.BlockSpec(tuple(shape), lambda i: (0,) * len(shape), pipeline_mode=pl.Buffered(1))
        return pl.BlockSpec((tile, shape[1]), lambda i: (first[kind](i), 0), **({"pipeline_mode": pl.Buffered(1)} if kind in "op" and shape[0] == tile else {}))

    cut = len(outs) - sums
    return pl.pallas_call(
        kernel,
        grid=(steps,),
        in_specs=[spec(kind, a.shape) for kind, a in args] + [pl.BlockSpec(memory_space=pl.ANY)] * len(weights),
        out_specs=[spec(kind, o.shape) for kind, o in outs[:cut]]
        + [pl.BlockSpec(o.shape, lambda i: (0, 0)) for _, o in outs[cut:]]
        + [pl.BlockSpec(memory_space=pl.ANY)] * len(far),
        out_shape=[in_hbm(o) for _, o in outs] + list(far),
        scratch_shapes=[pltpu.VMEM(w.shape[2:], BF16) for w in weights]
        + ([pltpu.SemaphoreType.DMA((2,))] if weights else [])
        + list(scratch),
        compiler_params=params(),
        cost_estimate=cost(),
        name=name,
    )(*(to_hbm(a) for _, a in args), *(pltpu.with_memory_space_constraint(w, pltpu.HBM) for w in weights))


def in_own_half():
    return pl.program_id(0) < pl.num_programs(0) // 2


def pick(own_ref, par_ref):
    return jnp.where(in_own_half(), own_ref[...], par_ref[...]).astype(F32)


def row_sum(v):
    return jnp.sum(v, axis=0, keepdims=True)


def vec(ref, layer):
    return ref[layer : layer + 1].astype(F32)


def slots_of(experts, capacity, routes):
    n = routes.shape[1]
    onehot = routes == lax.broadcasted_iota(jnp.int32, (experts, n), 0)
    hot = jnp.where(onehot, 1.0, 0.0)
    before = lax.broadcasted_iota(jnp.int32, (n, n), 0) < lax.broadcasted_iota(jnp.int32, (n, n), 1)
    earlier = dot_nn(hot.astype(BF16), jnp.where(before, 1.0, 0.0).astype(BF16))
    return routes * capacity + row_sum(earlier * hot).astype(jnp.int32)


def pack_first_kernel(experts, capacity, routes_ref, tokens_ref, out_ref, place_ref):
    slots = out_ref.shape[0]
    n = tokens_ref.shape[0]
    slot = slots_of(experts, capacity, routes_ref[...])
    hit = slot == lax.broadcasted_iota(jnp.int32, (slots, n), 0)
    hot = jnp.where(hit, 1.0, 0.0)
    place_ref[...] = hot.astype(BF16)
    packed = dot_nn(place_ref[...], tokens_ref[...])
    out_ref[...] = packed.astype(BF16)
    empty = 1.0 - jnp.sum(hot, axis=1, keepdims=True)
    out_ref[:, :128] = (packed[:, :128] + empty * PAD_MARK).astype(BF16)


def pack_kernel(place_ref, values_ref, out_ref):
    out_ref[...] = dot_nn(place_ref[...], values_ref[...]).astype(BF16)


def unpack_kernel(place_ref, returned_ref, base_ref, out_ref):
    picked = dot_tn(place_ref[...], returned_ref[...])
    out_ref[...] = (base_ref[...].astype(F32) + picked).astype(BF16)


class Weights:
    def __init__(self, layer, refs, order):
        first, second, self.bufs, self.sems = refs[0], refs[1], refs[2:4], refs[4]
        self.copies = [
            pltpu.make_async_copy(ref.at[layer, 0], self.bufs[k], self.sems.at[k]) for k, ref in enumerate((first, second))
        ]

        @pl.when(pl.program_id(0) == 0)
        def _():
            for k in order:
                self.copies[k].start()

    def take(self, k):
        @pl.when(pl.program_id(0) == 0)
        def _():
            self.copies[k].wait()

        return self.bufs[k][...]


def norm_stats(h):
    mu = jnp.mean(h, axis=1, keepdims=True)
    c = h - mu
    r = lax.rsqrt(jnp.mean(c * c, axis=1, keepdims=True) + EPS)
    return mu, r, c * r


def feed_forward(layer, low, weights, b_in_ref, act_ref, slope_ref):
    hidden = dot_nn(low, weights.take(0)) + vec(b_in_ref, layer)
    act, slope = gelu_and_slope(hidden)
    act = act.astype(BF16)
    act_ref[...] = act
    slope_ref[...] = slope.astype(BF16)
    return dot_nn(act, weights.take(1))


def first_kernel(
    own_ref, par_ref, gain_ref, shift_ref, center_ref, b_in_ref, w_in_ref, w_out_ref,
    low_ref, act_ref, slope_ref, part_ref, row_ref, *bufs,
):
    weights = Weights(0, (w_in_ref, w_out_ref, *bufs), (0, 1))
    x = pick(own_ref, par_ref)
    mu, r, xhat = norm_stats(x)
    low = (xhat * vec(gain_ref, 0) + vec(shift_ref, 0)).astype(BF16)
    low_ref[...] = low
    logit = jnp.sum(x * center_ref[...].astype(F32), axis=1, keepdims=True)
    gate = jax.nn.sigmoid(logit)
    live = jnp.where(x[:, :1] < PAD_LIMIT, 1.0, 0.0)
    lane = lax.broadcasted_iota(jnp.int32, row_ref.shape, 1)
    row_ref[...] = jnp.where(lane == 0, mu, jnp.where(lane == 1, r, jnp.where(lane == 2, gate, live)))
    part = feed_forward(0, low, weights, b_in_ref, act_ref, slope_ref)
    part_ref[...] = part.astype(BF16)


def branch_kernel(part_ref, theirs_ref, row_ref, out_ref, branch_ref):
    out = part_ref[...] + theirs_ref[...].astype(F32)
    out_ref[...] = out.astype(BF16)
    branch_ref[...] = (row_ref[:, 2:3] * out).astype(BF16)


def start_sums(sums_ref):
    @pl.when(pl.program_id(0) == 0)
    def _():
        sums_ref[...] = jnp.zeros_like(sums_ref)


def back_feed(ds, weights, slope_ref, dh_ref, sums_ref):
    depth = ds.shape[1]
    dact = dot_nt(ds, weights.take(1))
    dh = (dact * slope_ref[...].astype(F32)).astype(BF16)
    dh_ref[...] = dh
    bias = row_sum(dh.astype(F32))
    for j in range(bias.shape[1] // depth):
        sums_ref[3 + j : 4 + j] += bias[:, j * depth : (j + 1) * depth]
    return dot_nt(dh, weights.take(0))


def second_kernel(
    x_own_ref, x_par_ref, mine_ref, theirs_ref, dy_own_ref, dy_par_ref, gate_ref,
    b_out_ref, gain_ref, shift_ref, b_in_ref, w_in_ref, w_out_ref,
    part_own_ref, part_par_ref, xhat_ref, row_ref, back_ref, sums_ref, grad_in_ref, grad_out_ref,
    w_in_buf, w_out_buf, sems, low_ref, act_ref, slope_ref, ds_ref, dh_ref, sum_in_ref, sum_out_ref, out_sems,
):
    weights = Weights(1, (w_in_ref, w_out_ref, w_in_buf, w_out_buf, sems), (0, 1))
    start_sums(sums_ref)
    start_sums(sum_in_ref)
    start_sums(sum_out_ref)
    own = in_own_half()
    last = pl.program_id(0) == pl.num_programs(0) - 1
    depth, half = sum_in_ref.shape
    h = pick(x_own_ref, x_par_ref) + vec(b_out_ref, 0) + (mine_ref[...].astype(F32) + theirs_ref[...].astype(F32))
    mu, r, xhat = norm_stats(h)
    low_ref[...] = (xhat * vec(gain_ref, 1) + vec(shift_ref, 1)).astype(BF16)
    xhat_ref[...] = xhat.astype(BF16)
    row_ref[...] = jnp.broadcast_to(r, row_ref.shape)
    ds = gate_ref[:, 2:3] * pick(dy_own_ref, dy_par_ref)
    ds_ref[...] = ds.astype(BF16)

    @pl.when(own)
    def _():
        part_own_ref[...] = h + vec(b_out_ref, 1)

    part = feed_forward(1, low_ref[...], weights, b_in_ref, act_ref, slope_ref)

    @pl.when(own)
    def _():
        part_own_ref[...] += part

    @pl.when(jnp.logical_not(own))
    def _():
        part_par_ref[...] = part.astype(BF16)

    sum_out_ref[...] += dot_tn(act_ref[...], ds_ref[...])
    out_copy = pltpu.make_async_copy(sum_out_ref, grad_out_ref.at[1, 0], out_sems.at[0])
    pl.when(last)(out_copy.start)
    dact = dot_nt(ds_ref[...], w_out_buf[...])
    dh_ref[...] = (dact * slope_ref[...].astype(F32)).astype(BF16)
    bias = row_sum(dh_ref[...].astype(F32))
    for j in range(half // depth):
        sums_ref[3 + j : 4 + j] += bias[:, j * depth : (j + 1) * depth]
    in_copies = []
    for j in range(2):
        part = pl.ds(j * half // 2, half // 2)
        sum_in_ref[:, part] += dot_tn(low_ref[...], dh_ref[:, part])
        copy = pltpu.make_async_copy(sum_in_ref.at[:, part], grad_in_ref.at[1, 0, :, part], out_sems.at[1 + j])
        pl.when(last)(copy.start)
        in_copies.append(copy)
    dn = dot_nt(dh_ref[...], w_in_buf[...])
    back_ref[...] = dn.astype(BF16)
    sums_ref[0:1] += row_sum(dn * xhat)
    sums_ref[1:2] += row_sum(dn)
    sums_ref[2:3] += row_sum(ds_ref[...].astype(F32))

    @pl.when(last)
    def _():
        for copy in (out_copy, *in_copies):
            copy.wait()


def norm_back(dn, gain, xhat, r):
    dxhat = dn * gain
    m1 = jnp.mean(dxhat, axis=1, keepdims=True)
    m2 = jnp.mean(dxhat * xhat, axis=1, keepdims=True)
    return r * (dxhat - m1 - xhat * m2)


def back_first_kernel(
    own_ref, par_ref, row_ref, mine_ref, theirs_ref, xhat_ref, row1_ref, gain_ref, x_own_ref, x_par_ref, slope_ref,
    w_in_ref, w_out_ref, ds_ref, dh_ref, part_own_ref, carry_ref, part_par_ref, sums_ref, *bufs,
):
    weights = Weights(0, (w_in_ref, w_out_ref, *bufs), (1, 0))
    start_sums(sums_ref)
    own = in_own_half()
    dn = mine_ref[...].astype(F32) + theirs_ref[...].astype(F32)
    carry = row_ref[:, 2:3] * pick(own_ref, par_ref) + norm_back(
        dn, vec(gain_ref, 1), xhat_ref[...].astype(F32), row1_ref[:, 0:1]
    )
    ds = carry.astype(BF16)
    ds_ref[...] = ds

    @pl.when(own)
    def _():
        carry_ref[...] = carry

    dn = back_feed(ds, weights, slope_ref, dh_ref, sums_ref)
    xhat = (pick(x_own_ref, x_par_ref) - row_ref[:, 0:1]) * row_ref[:, 1:2]
    sums_ref[0:1] += row_sum(dn * xhat)
    sums_ref[1:2] += row_sum(dn)
    sums_ref[2:3] += row_sum(ds.astype(F32))

    @pl.when(own)
    def _():
        part_own_ref[...] = dn

    @pl.when(jnp.logical_not(own))
    def _():
        part_par_ref[...] = dn.astype(BF16)


def input_kernel(
    dy_ref, out_ref, row_ref, x_ref, part_ref, theirs_ref, carry_ref, gain_ref, center_ref, s0_ref, s1_ref,
    drow_ref, local_ref,
):
    @pl.when(pl.program_id(0) == 0)
    def _():
        local_ref[0:8] = s0_ref[...]
        local_ref[8:16] = s1_ref[...]
        local_ref[16:24] = jnp.zeros_like(local_ref[16:24])

    x = x_ref[...].astype(F32)
    gate = row_ref[:, 2:3]
    live = row_ref[:, 3:4]
    dgate = jnp.sum(dy_ref[...].astype(F32) * out_ref[...].astype(F32), axis=1, keepdims=True)
    dlogit = dgate * gate * (1.0 - gate)
    dn = part_ref[...] + theirs_ref[...].astype(F32)
    r = row_ref[:, 1:2]
    carry = carry_ref[...] + norm_back(dn, vec(gain_ref, 0), (x - row_ref[:, 0:1]) * r, r)
    drow_ref[...] = (carry + dlogit * center_ref[...].astype(F32)).astype(BF16)
    local_ref[16:17] += row_sum(dlogit * x)
    local_ref[17:18] += jnp.broadcast_to(row_sum(gate * live), (1, x.shape[1]))
    local_ref[18:19] += jnp.broadcast_to(row_sum(live), (1, x.shape[1]))


def finish_kernel(
    mean_load, here_ref, local_ref, other_ref, b_in_ref, b_out_ref, gain_ref, shift_ref, center_ref, gate_ref, load_ref
):
    depth = local_ref.shape[1]
    for layer in range(2):
        base = 8 * layer
        gain_ref[layer] = local_ref[base : base + 1] + other_ref[base : base + 1]
        shift_ref[layer] = local_ref[base + 1 : base + 2] + other_ref[base + 1 : base + 2]
        b_out_ref[layer] = local_ref[base + 2 : base + 3]
        parts = b_in_ref.shape[2] // (2 * depth)
        for side in range(2):

            @pl.when(here_ref[0] == side)
            def _():
                for j in range(parts):
                    low = (side * parts + j) * depth
                    b_in_ref[layer, :, low : low + depth] = local_ref[base + 3 + j : base + 4 + j]
                    low = ((1 - side) * parts + j) * depth
                    b_in_ref[layer, :, low : low + depth] = other_ref[base + 3 + j : base + 4 + j]

    total = local_ref[16:24] + other_ref[16:24]
    center_ref[...] = total[0:1]
    gate_ref[...] = total[1:2, :128] / total[2:3, :128]
    load_ref[...] = total[2:3, :128] / mean_load


def weight_kernel(by_left, moving_ref, fixed_ref, _, out_ref):
    if by_left:
        out_ref[...] = dot_tn(moving_ref[...], fixed_ref[...])
    else:
        out_ref[...] = dot_tn(fixed_ref[...], moving_ref[...])


def weight_gradient(by_left, moving, fixed, into, blk):
    rows, width = moving.shape
    other = fixed.shape[1]
    if by_left:
        out_spec = pl.BlockSpec((None, None, blk, other), lambda i: (0, 0, i, 0))
    else:
        out_spec = pl.BlockSpec((None, None, other, blk), lambda i: (0, 0, 0, i))
    return pl.pallas_call(
        lambda *refs: weight_kernel(by_left, *refs),
        grid=(width // blk,),
        in_specs=[
            pl.BlockSpec((rows, blk), lambda i: (0, i)),
            pl.BlockSpec((rows, other), lambda i: (0, 0), pipeline_mode=pl.Buffered(1)),
            pl.BlockSpec(memory_space=pl.ANY),
        ],
        out_specs=out_spec,
        out_shape=sds(into.shape, F32),
        input_output_aliases={2: 0},
        compiler_params=params(),
        cost_estimate=cost(),
        name="weight_gradient",
    )(to_hbm(moving), to_hbm(fixed), into)


def on_device(tokens, routes, cotangent, ln_gain, ln_shift, w_in, b_in, w_out, b_out, centroid):
    experts = lax.axis_size("expert")
    replicas = lax.axis_size("replica")
    here = lax.axis_index("replica")
    tok_dev, depth = tokens.shape
    half = w_in.shape[3]
    capacity = 2 * tok_dev // experts
    slots = experts * capacity
    both = 2 * slots
    gain, shift, b_out = (v.reshape(2, depth) for v in (ln_gain, ln_shift, b_out))

    def exchange(v):
        moved = lax.all_to_all(
            v.reshape(experts, capacity, depth), "expert", split_axis=0, concat_axis=0, tiled=True
        )
        return moved.reshape(slots, depth)

    def swap(v):
        return lax.ppermute(v, "replica", SWAP)

    sent_tok, place = call(
        lambda *refs: pack_first_kernel(experts, capacity, *refs),
        "pack_first",
        (routes.reshape(1, tok_dev), tokens),
        [sds((slots, depth), BF16), sds((slots, tok_dev), BF16)],
    )
    b_half = lax.dynamic_slice_in_dim(b_in.reshape(2, 2 * half), here * half, half, axis=1)
    x_own = exchange(sent_tok)
    x_par = swap(x_own)
    [sent_cot] = call(pack_kernel, "pack", (place, cotangent), [sds((slots, depth), BF16)])
    sent_cot, x_own = lax.optimization_barrier((sent_cot, x_own))
    dy_own = exchange(sent_cot)

    narrow, wide = ("r", sds((both, depth), BF16)), ("r", sds((both, half), BF16))
    per_row = ("r", sds((both, 128), F32))
    own_sum, par_sum = ("o", sds((slots, depth), F32)), ("p", sds((slots, depth), BF16))
    sums = ("w", sds((8, depth), F32))
    x = (("o", x_own), ("p", x_par))
    low0, act0, slope0, p0, row = row_call(
        first_kernel,
        "forward_first",
        both,
        (*x, ("w", gain), ("w", shift), ("w", centroid), ("w", b_half)),
        [narrow, wide, wide, narrow, per_row],
        weights=(w_in, w_out),
        tile=256,
    )
    dy = (("o", dy_own), ("p", swap(dy_own)))
    p1_own, p1_par, xhat1, row1, n1, sums1, grad_in, grad_out = row_call(
        second_kernel,
        "second",
        both,
        (
            *x, ("r", p0), ("s", swap(p0)), *dy, ("r", row),
            ("w", b_out), ("w", gain), ("w", shift), ("w", b_half),
        ),
        [own_sum, par_sum, narrow, per_row, narrow, sums],
        sums=1,
        weights=(w_in, w_out),
        tile=256,
        far=(sds((2, 1, depth, half), F32), sds((2, 1, half, depth), F32)),
        scratch=[
            pltpu.VMEM((256, depth), BF16),
            pltpu.VMEM((256, half), BF16),
            pltpu.VMEM((256, half), BF16),
            pltpu.VMEM((256, depth), BF16),
            pltpu.VMEM((256, half), BF16),
            pltpu.VMEM((depth, half), F32),
            pltpu.VMEM((half, depth), F32),
            pltpu.SemaphoreType.DMA((3,)),
        ],
    )
    p1_there, n1 = lax.optimization_barrier((swap(p1_par), n1))
    out, branch = row_call(
        branch_kernel,
        "branch",
        slots,
        (("r", p1_own), ("r", p1_there), ("r", row)),
        [("r", sds((slots, depth), BF16))] * 2,
        tile=256,
    )
    returned = exchange(branch)
    ds0, dh0, n0_own, carry_own, n0_par, sums0 = row_call(
        back_first_kernel,
        "backward_first",
        both,
        (
            *dy, ("r", row), ("r", n1), ("s", swap(n1)), ("r", xhat1), ("r", row1), ("w", gain), *x, ("r", slope0),
        ),
        [narrow, wide, own_sum, own_sum, par_sum, sums],
        sums=1,
        tile=256,
        weights=(w_in, w_out),
    )
    drow, local = row_call(
        input_kernel,
        "input_gradient",
        slots,
        (
            ("r", dy_own), ("r", out), ("r", row), ("r", x_own), ("r", n0_own), ("r", swap(n0_par)), ("r", carry_own),
            ("w", gain), ("w", centroid), ("w", sums0), ("w", sums1),
        ),
        [("r", sds((slots, depth), BF16)), ("w", sds((24, depth), F32))],
        sums=1,
        tile=256,
    )
    drow, returned = lax.optimization_barrier((drow, returned))
    grad_returned = exchange(drow)

    grad_out = weight_gradient(True, act0, ds0, grad_out, 512)
    grad_in = weight_gradient(False, dh0, low0, grad_in, 512)
    [mixed] = call(unpack_kernel, "unpack", (place, returned, tokens), [sds(tokens.shape, BF16)])
    other = swap(local)
    one = sds((2, 1, depth), F32)
    grad_b_in, grad_b_out, grad_gain, grad_shift, grad_center, mean_gate, load = call(
        lambda *refs: finish_kernel(float(tok_dev * replicas), *refs),
        "finish",
        (here.astype(jnp.int32).reshape(1), local, other),
        [sds((2, 1, 2 * half), F32), one, one, one, sds((1, depth), F32), sds((1, 128), F32), sds((1, 128), F32)],
        smem_in=1,
    )
    [grad_tokens] = call(unpack_kernel, "unpack", (place, grad_returned, cotangent), [sds(tokens.shape, BF16)])
    return (
        mixed, grad_tokens, grad_in, grad_out, grad_b_in, grad_b_out, grad_gain, grad_shift, grad_center,
        mean_gate[0, :1], load[0, :1],
    )


def solution(mesh):
    rows = P(("expert", "replica"), None)
    by_expert = P(None, "expert", None)
    first_weight = P(None, "expert", None, "replica")
    second_weight = P(None, "expert", "replica", None)
    return jax.shard_map(
        on_device,
        mesh=mesh,
        in_specs=(
            rows, rows, rows, by_expert, by_expert, first_weight, by_expert, second_weight, by_expert,
            P("expert", None),
        ),
        out_specs=(
            rows, rows, first_weight, second_weight, by_expert, by_expert, by_expert, by_expert,
            P("expert", None), P("expert"), P("expert"),
        ),
        check_vma=False,
    )
```

```python
import jax
import jax.numpy as jnp
from jax import lax
from jax.experimental import pallas as pl
from jax.experimental.pallas import tpu as pltpu
from jax.sharding import PartitionSpec as P

EPS = 1e-05
F32 = jnp.float32
BF16 = jnp.bfloat16
PAD_MARK = 64.0
PAD_LIMIT = 32.0
SWAP = [(0, 1), (1, 0)]
VMEM = pl.BlockSpec(memory_space=pltpu.VMEM)
SMEM = pl.BlockSpec(memory_space=pltpu.SMEM)


def dot_nn(a, b):
    return lax.dot_general(a, b, (((1,), (0,)), ((), ())), preferred_element_type=F32)


def dot_nt(a, b):
    return lax.dot_general(a, b, (((1,), (1,)), ((), ())), preferred_element_type=F32)


def dot_tn(a, b):
    return lax.dot_general(a, b, (((0,), (0,)), ((), ())), preferred_element_type=F32)


def gelu_and_slope(v):
    phi = 0.5 + 0.5 * lax.erf(v * 0.7071067811865476)
    return v * phi, phi + v * (jnp.exp(v * v * -0.5) * 0.3989422804014327)


def sds(shape, dtype):
    return jax.ShapeDtypeStruct(shape, dtype)


def large(a):
    return len(a.shape) > 1 and a.shape[0] * a.shape[1] >= 1 << 16


def to_hbm(a):
    return pltpu.with_memory_space_constraint(a, pltpu.HBM) if large(a) else a


def in_hbm(o):
    return pltpu.HBM(o.shape, o.dtype) if large(o) else o


def cost():
    return pl.CostEstimate(flops=0, bytes_accessed=0, transcendentals=0)


def params(mib=52):
    return pltpu.CompilerParams(vmem_limit_bytes=mib << 20)


def call(kernel, name, args, outs, smem_in=0):
    return pl.pallas_call(
        kernel,
        in_specs=[SMEM] * smem_in + [VMEM] * (len(args) - smem_in),
        out_specs=[VMEM] * len(outs),
        out_shape=outs,
        compiler_params=params(),
        cost_estimate=cost(),
        name=name,
    )(*args)


def row_call(kernel, name, rows, args, outs, sums=0, weights=(), far=(), scratch=(), tile=256, mib=52):
    steps = rows // tile
    half = steps // 2
    first = {
        "r": lambda i: i,
        "o": lambda i: jnp.minimum(i, half - 1),
        "p": lambda i: jnp.maximum(i - half, 0),
        "s": lambda i: lax.rem(i + half, steps),
    }

    def spec(kind, shape):
        if kind == "w":
            return pl.BlockSpec(tuple(shape), lambda i: (0,) * len(shape), pipeline_mode=pl.Buffered(1))
        return pl.BlockSpec((tile, shape[1]), lambda i: (first[kind](i), 0), **({"pipeline_mode": pl.Buffered(1)} if kind in "op" and shape[0] == tile else {}))

    cut = len(outs) - sums
    return pl.pallas_call(
        kernel,
        grid=(steps,),
        in_specs=[spec(kind, a.shape) for kind, a in args] + [pl.BlockSpec(memory_space=pl.ANY)] * len(weights),
        out_specs=[spec(kind, o.shape) for kind, o in outs[:cut]]
        + [pl.BlockSpec(o.shape, lambda i: (0, 0)) for _, o in outs[cut:]]
        + [pl.BlockSpec(memory_space=pl.ANY)] * len(far),
        out_shape=[in_hbm(o) for _, o in outs] + list(far),
        scratch_shapes=[pltpu.VMEM(w.shape[2:], BF16) for w in weights]
        + ([pltpu.SemaphoreType.DMA((2,))] if weights else [])
        + list(scratch),
        compiler_params=params(mib),
        cost_estimate=cost(),
        name=name,
    )(*(to_hbm(a) if weights and kind != "p" else a for kind, a in args), *(pltpu.with_memory_space_constraint(w, pltpu.HBM) for w in weights))


def in_own_half():
    return pl.program_id(0) < pl.num_programs(0) // 2


def pick(own_ref, par_ref):
    return jnp.where(in_own_half(), own_ref[...], par_ref[...]).astype(F32)


def row_sum(v):
    return jnp.sum(v, axis=0, keepdims=True)


def vec(ref, layer):
    return ref[layer : layer + 1].astype(F32)


def slots_of(experts, capacity, routes):
    n = routes.shape[1]
    onehot = routes == lax.broadcasted_iota(jnp.int32, (experts, n), 0)
    hot = jnp.where(onehot, 1.0, 0.0)
    before = lax.broadcasted_iota(jnp.int32, (n, n), 0) < lax.broadcasted_iota(jnp.int32, (n, n), 1)
    earlier = dot_nn(hot.astype(BF16), jnp.where(before, 1.0, 0.0).astype(BF16))
    return routes * capacity + row_sum(earlier * hot).astype(jnp.int32)


def pack_first_kernel(experts, capacity, routes_ref, tokens_ref, out_ref, place_ref):
    slots = out_ref.shape[0]
    n = tokens_ref.shape[0]
    slot = slots_of(experts, capacity, routes_ref[...])
    hit = slot == lax.broadcasted_iota(jnp.int32, (slots, n), 0)
    hot = jnp.where(hit, 1.0, 0.0)
    place_ref[...] = hot.astype(BF16)
    packed = dot_nn(place_ref[...], tokens_ref[...])
    out_ref[...] = packed.astype(BF16)
    empty = 1.0 - jnp.sum(hot, axis=1, keepdims=True)
    out_ref[:, :128] = (packed[:, :128] + empty * PAD_MARK).astype(BF16)


def pack_kernel(place_ref, values_ref, out_ref):
    out_ref[...] = dot_nn(place_ref[...], values_ref[...]).astype(BF16)


def unpack_kernel(place_ref, returned_ref, base_ref, out_ref):
    picked = dot_tn(place_ref[...], returned_ref[...])
    out_ref[...] = (base_ref[...].astype(F32) + picked).astype(BF16)


class Weights:
    def __init__(self, layer, refs, order):
        first, second, self.bufs, self.sems = refs[0], refs[1], refs[2:4], refs[4]
        self.copies = [
            pltpu.make_async_copy(ref.at[layer, 0], self.bufs[k], self.sems.at[k]) for k, ref in enumerate((first, second))
        ]

        @pl.when(pl.program_id(0) == 0)
        def _():
            for k in order:
                self.copies[k].start()

    def take(self, k):
        @pl.when(pl.program_id(0) == 0)
        def _():
            self.copies[k].wait()

        return self.bufs[k][...]


def norm_stats(h):
    mu = jnp.mean(h, axis=1, keepdims=True)
    c = h - mu
    r = lax.rsqrt(jnp.mean(c * c, axis=1, keepdims=True) + EPS)
    return mu, r, c * r


def feed_forward(layer, low, weights, b_in_ref, act_ref, slope_ref):
    hidden = dot_nn(low, weights.take(0)) + vec(b_in_ref, layer)
    act, slope = gelu_and_slope(hidden)
    act = act.astype(BF16)
    act_ref[...] = act
    slope_ref[...] = slope.astype(BF16)
    return dot_nn(act, weights.take(1))


def first_kernel(
    own_ref, par_ref, gain_ref, shift_ref, center_ref, b_in_ref, w_in_ref, w_out_ref,
    low_ref, act_ref, slope_ref, part_ref, row_ref, *bufs,
):
    weights = Weights(0, (w_in_ref, w_out_ref, *bufs), (0, 1))
    x = pick(own_ref, par_ref)
    mu, r, xhat = norm_stats(x)
    low = (xhat * vec(gain_ref, 0) + vec(shift_ref, 0)).astype(BF16)
    low_ref[...] = low
    logit = jnp.sum(x * center_ref[...].astype(F32), axis=1, keepdims=True)
    gate = jax.nn.sigmoid(logit)
    live = jnp.where(x[:, :1] < PAD_LIMIT, 1.0, 0.0)
    lane = lax.broadcasted_iota(jnp.int32, row_ref.shape, 1)
    row_ref[...] = jnp.where(lane == 0, mu, jnp.where(lane == 1, r, jnp.where(lane == 2, gate, live)))
    part = feed_forward(0, low, weights, b_in_ref, act_ref, slope_ref)
    part_ref[...] = part.astype(BF16)


def branch_kernel(part_ref, theirs_ref, row_ref, out_ref, branch_ref):
    out = part_ref[...] + theirs_ref[...].astype(F32)
    out_ref[...] = out.astype(BF16)
    branch_ref[...] = (row_ref[:, 2:3] * out).astype(BF16)


def start_sums(sums_ref):
    @pl.when(pl.program_id(0) == 0)
    def _():
        sums_ref[...] = jnp.zeros_like(sums_ref)


def back_feed(ds, weights, slope_ref, dh_ref, sums_ref):
    depth = ds.shape[1]
    dact = dot_nt(ds, weights.take(1))
    dh = (dact * slope_ref[...].astype(F32)).astype(BF16)
    dh_ref[...] = dh
    bias = row_sum(dh.astype(F32))
    for j in range(bias.shape[1] // depth):
        sums_ref[3 + j : 4 + j] += bias[:, j * depth : (j + 1) * depth]
    return dot_nt(dh, weights.take(0))


def second_kernel(
    x_own_ref, x_par_ref, mine_ref, theirs_ref, dy_own_ref, dy_par_ref, gate_ref,
    b_out_ref, gain_ref, shift_ref, b_in_ref, w_in_ref, w_out_ref,
    part_own_ref, part_par_ref, xhat_ref, row_ref, back_ref, low_ref, later_ref, sums_ref, grad_in_ref, grad_out_ref,
    w_in_buf, w_out_buf, sems, act_ref, slope_ref, ds_ref, dh_ref, sum_in_ref, sum_out_ref, out_sems,
):
    weights = Weights(1, (w_in_ref, w_out_ref, w_in_buf, w_out_buf, sems), (0, 1))
    start_sums(sums_ref)
    start_sums(sum_in_ref)
    start_sums(sum_out_ref)
    own = in_own_half()
    last = pl.program_id(0) == pl.num_programs(0) - 1
    half, depth = sum_out_ref.shape
    now = sum_in_ref.shape[1]
    h = pick(x_own_ref, x_par_ref) + vec(b_out_ref, 0) + (mine_ref[...].astype(F32) + theirs_ref[...].astype(F32))
    mu, r, xhat = norm_stats(h)
    low_ref[...] = (xhat * vec(gain_ref, 1) + vec(shift_ref, 1)).astype(BF16)
    xhat_ref[...] = xhat.astype(BF16)
    row_ref[...] = jnp.broadcast_to(r, row_ref.shape)
    ds = gate_ref[:, 2:3] * pick(dy_own_ref, dy_par_ref)
    ds_ref[...] = ds.astype(BF16)

    @pl.when(own)
    def _():
        part_own_ref[...] = h + vec(b_out_ref, 1)

    part = feed_forward(1, low_ref[...], weights, b_in_ref, act_ref, slope_ref)

    @pl.when(own)
    def _():
        part_own_ref[...] += part

    @pl.when(jnp.logical_not(own))
    def _():
        part_par_ref[...] = part.astype(BF16)

    sum_out_ref[...] += dot_tn(act_ref[...], ds_ref[...])
    out_copy = pltpu.make_async_copy(sum_out_ref, grad_out_ref.at[1, 0], out_sems.at[0])
    pl.when(last)(out_copy.start)
    dact = dot_nt(ds_ref[...], w_out_buf[...])
    dh_ref[...] = (dact * slope_ref[...].astype(F32)).astype(BF16)
    bias = row_sum(dh_ref[...].astype(F32))
    for j in range(half // depth):
        sums_ref[3 + j : 4 + j] += bias[:, j * depth : (j + 1) * depth]
    sum_in_ref[...] += dot_tn(low_ref[...], dh_ref[:, :now])
    later_ref[...] = dh_ref[:, now:]
    in_copy = pltpu.make_async_copy(sum_in_ref, grad_in_ref.at[1, 0, :, pl.ds(0, now)], out_sems.at[1])
    pl.when(last)(in_copy.start)
    dn = dot_nt(dh_ref[...], w_in_buf[...])
    back_ref[...] = dn.astype(BF16)
    sums_ref[0:1] += row_sum(dn * xhat)
    sums_ref[1:2] += row_sum(dn)
    sums_ref[2:3] += row_sum(ds_ref[...].astype(F32))

    @pl.when(last)
    def _():
        out_copy.wait()
        in_copy.wait()


def norm_back(dn, gain, xhat, r):
    dxhat = dn * gain
    m1 = jnp.mean(dxhat, axis=1, keepdims=True)
    m2 = jnp.mean(dxhat * xhat, axis=1, keepdims=True)
    return r * (dxhat - m1 - xhat * m2)


def back_first_kernel(
    own_ref, par_ref, row_ref, mine_ref, theirs_ref, xhat_ref, row1_ref, gain_ref, x_own_ref, x_par_ref, slope_ref,
    w_in_ref, w_out_ref, ds_ref, dh_ref, part_own_ref, carry_ref, part_par_ref, sums_ref, *bufs,
):
    weights = Weights(0, (w_in_ref, w_out_ref, *bufs), (1, 0))
    start_sums(sums_ref)
    own = in_own_half()
    dn = mine_ref[...].astype(F32) + theirs_ref[...].astype(F32)
    carry = row_ref[:, 2:3] * pick(own_ref, par_ref) + norm_back(
        dn, vec(gain_ref, 1), xhat_ref[...].astype(F32), row1_ref[:, 0:1]
    )
    ds = carry.astype(BF16)
    ds_ref[...] = ds

    @pl.when(own)
    def _():
        carry_ref[...] = carry

    dn = back_feed(ds, weights, slope_ref, dh_ref, sums_ref)
    xhat = (pick(x_own_ref, x_par_ref) - row_ref[:, 0:1]) * row_ref[:, 1:2]
    sums_ref[0:1] += row_sum(dn * xhat)
    sums_ref[1:2] += row_sum(dn)
    sums_ref[2:3] += row_sum(ds.astype(F32))

    @pl.when(own)
    def _():
        part_own_ref[...] = dn.astype(BF16)

    @pl.when(jnp.logical_not(own))
    def _():
        part_par_ref[...] = dn.astype(BF16)


def input_kernel(
    dy_ref, out_ref, row_ref, x_ref, part_ref, theirs_ref, carry_ref, gain_ref, center_ref, s0_ref, s1_ref,
    drow_ref, local_ref,
):
    @pl.when(pl.program_id(0) == 0)
    def _():
        local_ref[0:8] = s0_ref[...]
        local_ref[8:16] = s1_ref[...]
        local_ref[16:24] = jnp.zeros_like(local_ref[16:24])

    x = x_ref[...].astype(F32)
    gate = row_ref[:, 2:3]
    live = row_ref[:, 3:4]
    dgate = jnp.sum(dy_ref[...].astype(F32) * out_ref[...].astype(F32), axis=1, keepdims=True)
    dlogit = dgate * gate * (1.0 - gate)
    dn = part_ref[...].astype(F32) + theirs_ref[...].astype(F32)
    r = row_ref[:, 1:2]
    carry = carry_ref[...] + norm_back(dn, vec(gain_ref, 0), (x - row_ref[:, 0:1]) * r, r)
    drow_ref[...] = (carry + dlogit * center_ref[...].astype(F32)).astype(BF16)
    local_ref[16:17] += row_sum(dlogit * x)
    local_ref[17:18] += jnp.broadcast_to(row_sum(gate * live), (1, x.shape[1]))
    local_ref[18:19] += jnp.broadcast_to(row_sum(live), (1, x.shape[1]))


def finish_kernel(
    mean_load, here_ref, local_ref, other_ref, b_in_ref, b_out_ref, gain_ref, shift_ref, center_ref, gate_ref, load_ref
):
    depth = local_ref.shape[1]
    for layer in range(2):
        base = 8 * layer
        gain_ref[layer] = local_ref[base : base + 1] + other_ref[base : base + 1]
        shift_ref[layer] = local_ref[base + 1 : base + 2] + other_ref[base + 1 : base + 2]
        b_out_ref[layer] = local_ref[base + 2 : base + 3]
        parts = b_in_ref.shape[2] // (2 * depth)
        for side in range(2):

            @pl.when(here_ref[0] == side)
            def _():
                for j in range(parts):
                    low = (side * parts + j) * depth
                    b_in_ref[layer, :, low : low + depth] = local_ref[base + 3 + j : base + 4 + j]
                    low = ((1 - side) * parts + j) * depth
                    b_in_ref[layer, :, low : low + depth] = other_ref[base + 3 + j : base + 4 + j]

    total = local_ref[16:24] + other_ref[16:24]
    center_ref[...] = total[0:1]
    gate_ref[...] = total[1:2, :128] / total[2:3, :128]
    load_ref[...] = total[2:3, :128] / mean_load


def out_kernel(act_ref, ds_ref, _, out_ref):
    out_ref[...] = dot_tn(act_ref[...], ds_ref[...])


def out_gradient(act, ds, into, blk):
    rows, half = act.shape
    depth = ds.shape[1]
    return pl.pallas_call(
        out_kernel,
        grid=(half // blk,),
        in_specs=[
            pl.BlockSpec((rows, blk), lambda i: (0, i)),
            pl.BlockSpec((rows, depth), lambda i: (0, 0), pipeline_mode=pl.Buffered(1)),
            pl.BlockSpec(memory_space=pl.ANY),
        ],
        out_specs=pl.BlockSpec((None, None, blk, depth), lambda i: (0, 0, i, 0)),
        out_shape=sds(into.shape, F32),
        input_output_aliases={2: 0},
        compiler_params=params(),
        cost_estimate=cost(),
        name="out_gradient",
    )(to_hbm(act), to_hbm(ds), into)


def in_kernel(first, low0_ref, dh0_ref, low1_ref, dh1_ref, _, out_ref):
    step = pl.program_id(0)

    @pl.when(step < first)
    def _():
        out_ref[...] = dot_tn(low0_ref[...], dh0_ref[...])

    @pl.when(step >= first)
    def _():
        out_ref[...] = dot_tn(low1_ref[...], dh1_ref[...])


def in_gradient(low0, dh0, low1, dh1, into, blk):
    rows, half = dh0.shape
    depth = low0.shape[1]
    first, steps = half // blk, (half + dh1.shape[1]) // blk
    skip = first - dh1.shape[1] // blk
    fixed = pl.BlockSpec((rows, depth), lambda i: (0, 0), pipeline_mode=pl.Buffered(1))
    return pl.pallas_call(
        lambda *refs: in_kernel(first, *refs),
        grid=(steps,),
        in_specs=[
            fixed,
            pl.BlockSpec((rows, blk), lambda i: (0, jnp.minimum(i, first - 1))),
            fixed,
            pl.BlockSpec((rows, blk), lambda i: (0, jnp.maximum(i - first, 0))),
            pl.BlockSpec(memory_space=pl.ANY),
        ],
        out_specs=pl.BlockSpec(
            (None, None, depth, blk),
            lambda i: (i // first, 0, 0, jnp.where(i < first, i, i - first + skip)),
        ),
        out_shape=sds(into.shape, F32),
        input_output_aliases={4: 0},
        compiler_params=params(),
        cost_estimate=cost(),
        name="in_gradient",
    )(*(to_hbm(v) for v in (low0, dh0, low1, dh1)), into)


def on_device(tokens, routes, cotangent, ln_gain, ln_shift, w_in, b_in, w_out, b_out, centroid):
    experts = lax.axis_size("expert")
    replicas = lax.axis_size("replica")
    here = lax.axis_index("replica")
    tok_dev, depth = tokens.shape
    half = w_in.shape[3]
    capacity = 2 * tok_dev // experts
    slots = experts * capacity
    both = 2 * slots
    gain, shift, b_out = (v.reshape(2, depth) for v in (ln_gain, ln_shift, b_out))

    def exchange(v):
        moved = lax.all_to_all(
            v.reshape(experts, capacity, depth), "expert", split_axis=0, concat_axis=0, tiled=True
        )
        return moved.reshape(slots, depth)

    def swap(v):
        return lax.ppermute(v, "replica", SWAP)

    sent_tok, place = call(
        lambda *refs: pack_first_kernel(experts, capacity, *refs),
        "pack_first",
        (routes.reshape(1, tok_dev), tokens),
        [sds((slots, depth), BF16), sds((slots, tok_dev), BF16)],
    )
    b_half = lax.dynamic_slice_in_dim(b_in.reshape(2, 2 * half), here * half, half, axis=1)
    x_own = exchange(sent_tok)
    [sent_cot] = call(pack_kernel, "pack", (place, cotangent), [sds((slots, depth), BF16)])
    sent_cot, x_own = lax.optimization_barrier((sent_cot, x_own))
    x_par = swap(x_own)
    dy_own = exchange(sent_cot)

    narrow, wide = ("r", sds((both, depth), BF16)), ("r", sds((both, half), BF16))
    per_row = ("r", sds((both, 128), F32))
    own_sum, par_sum = ("o", sds((slots, depth), F32)), ("p", sds((slots, depth), BF16))
    sums = ("w", sds((8, depth), F32))
    x = (("o", x_own), ("p", x_par))
    low0, act0, slope0, p0, row = row_call(
        first_kernel,
        "forward_first",
        both,
        (*x, ("w", gain), ("w", shift), ("w", centroid), ("w", b_half)),
        [narrow, wide, wide, narrow, per_row],
        weights=(w_in, w_out),
        tile=256,
    )
    dy = (("o", dy_own), ("p", swap(dy_own)))
    p1_own, p1_par, xhat1, row1, n1, low1, dh1, sums1, grad_in, grad_out = row_call(
        second_kernel,
        "second",
        both,
        (
            *x, ("r", p0), ("s", swap(p0)), *dy, ("r", row),
            ("w", b_out), ("w", gain), ("w", shift), ("w", b_half),
        ),
        [own_sum, par_sum, narrow, per_row, narrow, narrow, ("r", sds((both, half // 2), BF16)), sums],
        sums=1,
        weights=(w_in, w_out),
        mib=46,
        far=(sds((2, 1, depth, half), F32), sds((2, 1, half, depth), F32)),
        scratch=[
            pltpu.VMEM((256, half), BF16),
            pltpu.VMEM((256, half), BF16),
            pltpu.VMEM((256, depth), BF16),
            pltpu.VMEM((256, half), BF16),
            pltpu.VMEM((depth, half // 2), F32),
            pltpu.VMEM((half, depth), F32),
            pltpu.SemaphoreType.DMA((2,)),
        ],
    )
    p1_there, n1 = lax.optimization_barrier((swap(p1_par), n1))
    out, branch = row_call(
        branch_kernel,
        "branch",
        slots,
        (("r", p1_own), ("r", p1_there), ("r", row)),
        [("r", sds((slots, depth), BF16))] * 2,
        mib=24,
    )
    returned = exchange(branch)
    ds0, dh0, n0_own, carry_own, n0_par, sums0 = row_call(
        back_first_kernel,
        "backward_first",
        both,
        (
            *dy, ("r", row), ("r", n1), ("s", swap(n1)), ("r", xhat1), ("r", row1), ("w", gain), *x, ("r", slope0),
        ),
        [narrow, wide, ("o", sds((slots, depth), BF16)), own_sum, par_sum, sums],
        sums=1,
        tile=256,
        weights=(w_in, w_out),
    )
    drow, local = row_call(
        input_kernel,
        "input_gradient",
        slots,
        (
            ("r", dy_own), ("r", out), ("r", row), ("r", x_own), ("r", n0_own), ("r", swap(n0_par)), ("r", carry_own),
            ("w", gain), ("w", centroid), ("w", sums0), ("w", sums1),
        ),
        [("r", sds((slots, depth), BF16)), ("w", sds((24, depth), F32))],
        sums=1,
        mib=24,
    )
    drow, returned = lax.optimization_barrier((drow, returned))
    grad_returned = exchange(drow)

    grad_out = out_gradient(act0, ds0, grad_out, 512)
    grad_in = in_gradient(low0, dh0, low1, dh1, grad_in, 512)
    [mixed] = call(unpack_kernel, "unpack", (place, returned, tokens), [sds(tokens.shape, BF16)])
    other = swap(local)
    one = sds((2, 1, depth), F32)
    grad_b_in, grad_b_out, grad_gain, grad_shift, grad_center, mean_gate, load = call(
        lambda *refs: finish_kernel(float(tok_dev * replicas), *refs),
        "finish",
        (here.astype(jnp.int32).reshape(1), local, other),
        [sds((2, 1, 2 * half), F32), one, one, one, sds((1, depth), F32), sds((1, 128), F32), sds((1, 128), F32)],
        smem_in=1,
    )
    [grad_tokens] = call(unpack_kernel, "unpack", (place, grad_returned, cotangent), [sds(tokens.shape, BF16)])
    return (
        mixed, grad_tokens, grad_in, grad_out, grad_b_in, grad_b_out, grad_gain, grad_shift, grad_center,
        mean_gate[0, :1], load[0, :1],
    )


def solution(mesh):
    rows = P(("expert", "replica"), None)
    by_expert = P(None, "expert", None)
    first_weight = P(None, "expert", None, "replica")
    second_weight = P(None, "expert", "replica", None)
    return jax.shard_map(
        on_device,
        mesh=mesh,
        in_specs=(
            rows, rows, rows, by_expert, by_expert, first_weight, by_expert, second_weight, by_expert,
            P("expert", None),
        ),
        out_specs=(
            rows, rows, first_weight, second_weight, by_expert, by_expert, by_expert, by_expert,
            P("expert", None), P("expert"), P("expert"),
        ),
        check_vma=False,
    )
```

```python
import jax
import jax.numpy as jnp
from jax import lax
from jax.experimental import pallas as pl
from jax.experimental.pallas import tpu as pltpu
from jax.sharding import PartitionSpec as P

EPS = 1e-05
F32 = jnp.float32
BF16 = jnp.bfloat16
PAD_MARK = 64.0
PAD_LIMIT = 32.0
SWAP = [(0, 1), (1, 0)]
VMEM = pl.BlockSpec(memory_space=pltpu.VMEM)
SMEM = pl.BlockSpec(memory_space=pltpu.SMEM)


def dot_nn(a, b):
    return lax.dot_general(a, b, (((1,), (0,)), ((), ())), preferred_element_type=F32)


def dot_nt(a, b):
    return lax.dot_general(a, b, (((1,), (1,)), ((), ())), preferred_element_type=F32)


def dot_tn(a, b):
    return lax.dot_general(a, b, (((0,), (0,)), ((), ())), preferred_element_type=F32)


def gelu_and_slope(v):
    phi = 0.5 + 0.5 * lax.erf(v * 0.7071067811865476)
    return v * phi, phi + v * (jnp.exp(v * v * -0.5) * 0.3989422804014327)


def sds(shape, dtype):
    return jax.ShapeDtypeStruct(shape, dtype)


def large(a):
    return len(a.shape) > 1 and a.shape[0] * a.shape[1] >= 1 << 16


def to_hbm(a):
    return pltpu.with_memory_space_constraint(a, pltpu.HBM) if large(a) else a


def in_hbm(o):
    return pltpu.HBM(o.shape, o.dtype) if large(o) else o


def cost():
    return pl.CostEstimate(flops=0, bytes_accessed=0, transcendentals=0)


def params(mib=52):
    return pltpu.CompilerParams(vmem_limit_bytes=mib << 20)


def call(kernel, name, args, outs, smem_in=0):
    return pl.pallas_call(
        kernel,
        in_specs=[SMEM] * smem_in + [VMEM] * (len(args) - smem_in),
        out_specs=[VMEM] * len(outs),
        out_shape=outs,
        compiler_params=params(),
        cost_estimate=cost(),
        name=name,
    )(*args)


def row_call(kernel, name, rows, args, outs, sums=0, weights=(), far=(), scratch=(), tile=256, mib=52):
    steps = rows // tile
    half = steps // 2
    first = {
        "r": lambda i: i,
        "o": lambda i: jnp.minimum(i, half - 1),
        "p": lambda i: jnp.maximum(i - half, 0),
        "s": lambda i: lax.rem(i + half, steps),
    }

    def spec(kind, shape):
        if kind == "w":
            return pl.BlockSpec(tuple(shape), lambda i: (0,) * len(shape), pipeline_mode=pl.Buffered(1))
        return pl.BlockSpec((tile, shape[1]), lambda i: (first[kind](i), 0), **({"pipeline_mode": pl.Buffered(1)} if kind in "op" and shape[0] == tile else {}))

    cut = len(outs) - sums
    return pl.pallas_call(
        kernel,
        grid=(steps,),
        in_specs=[spec(kind, a.shape) for kind, a in args] + [pl.BlockSpec(memory_space=pl.ANY)] * len(weights),
        out_specs=[spec(kind, o.shape) for kind, o in outs[:cut]]
        + [pl.BlockSpec(o.shape, lambda i: (0, 0)) for _, o in outs[cut:]]
        + [pl.BlockSpec(memory_space=pl.ANY)] * len(far),
        out_shape=[in_hbm(o) for _, o in outs] + list(far),
        scratch_shapes=[pltpu.VMEM(w.shape[2:], BF16) for w in weights]
        + ([pltpu.SemaphoreType.DMA((2,))] if weights else [])
        + list(scratch),
        compiler_params=params(mib),
        cost_estimate=cost(),
        name=name,
    )(*(to_hbm(a) if weights and kind != "p" else a for kind, a in args), *(pltpu.with_memory_space_constraint(w, pltpu.HBM) for w in weights))


def in_own_half():
    return pl.program_id(0) < pl.num_programs(0) // 2


def pick(own_ref, par_ref):
    return jnp.where(in_own_half(), own_ref[...], par_ref[...]).astype(F32)


def row_sum(v):
    return jnp.sum(v, axis=0, keepdims=True)


def vec(ref, layer):
    return ref[layer : layer + 1].astype(F32)


def slots_of(experts, capacity, routes):
    n = routes.shape[1]
    onehot = routes == lax.broadcasted_iota(jnp.int32, (experts, n), 0)
    hot = jnp.where(onehot, 1.0, 0.0)
    before = lax.broadcasted_iota(jnp.int32, (n, n), 0) < lax.broadcasted_iota(jnp.int32, (n, n), 1)
    earlier = dot_nn(hot.astype(BF16), jnp.where(before, 1.0, 0.0).astype(BF16))
    return routes * capacity + row_sum(earlier * hot).astype(jnp.int32)


def pack_first_kernel(experts, capacity, routes_ref, tokens_ref, out_ref, place_ref):
    slots = out_ref.shape[0]
    n = tokens_ref.shape[0]
    slot = slots_of(experts, capacity, routes_ref[...])
    hit = slot == lax.broadcasted_iota(jnp.int32, (slots, n), 0)
    hot = jnp.where(hit, 1.0, 0.0)
    place_ref[...] = hot.astype(BF16)
    packed = dot_nn(place_ref[...], tokens_ref[...])
    out_ref[...] = packed.astype(BF16)
    empty = 1.0 - jnp.sum(hot, axis=1, keepdims=True)
    out_ref[:, :128] = (packed[:, :128] + empty * PAD_MARK).astype(BF16)


def pack_kernel(place_ref, values_ref, out_ref):
    out_ref[...] = dot_nn(place_ref[...], values_ref[...]).astype(BF16)


def unpack_kernel(place_ref, returned_ref, base_ref, out_ref):
    picked = dot_tn(place_ref[...], returned_ref[...])
    out_ref[...] = (base_ref[...].astype(F32) + picked).astype(BF16)


class Weights:
    def __init__(self, layer, refs, order):
        first, second, self.bufs, self.sems = refs[0], refs[1], refs[2:4], refs[4]
        self.copies = [
            pltpu.make_async_copy(ref.at[layer, 0], self.bufs[k], self.sems.at[k]) for k, ref in enumerate((first, second))
        ]

        @pl.when(pl.program_id(0) == 0)
        def _():
            for k in order:
                self.copies[k].start()

    def take(self, k):
        @pl.when(pl.program_id(0) == 0)
        def _():
            self.copies[k].wait()

        return self.bufs[k][...]


def norm_stats(h):
    mu = jnp.mean(h, axis=1, keepdims=True)
    c = h - mu
    r = lax.rsqrt(jnp.mean(c * c, axis=1, keepdims=True) + EPS)
    return mu, r, c * r


def feed_forward(layer, low, weights, b_in_ref, act_ref, slope_ref):
    hidden = dot_nn(low, weights.take(0)) + vec(b_in_ref, layer)
    act, slope = gelu_and_slope(hidden)
    act = act.astype(BF16)
    act_ref[...] = act
    slope_ref[...] = slope.astype(BF16)
    return dot_nn(act, weights.take(1))


def first_kernel(
    own_ref, par_ref, gain_ref, shift_ref, center_ref, b_in_ref, w_in_ref, w_out_ref,
    low_ref, act_ref, slope_ref, part_ref, row_ref, *bufs,
):
    weights = Weights(0, (w_in_ref, w_out_ref, *bufs), (0, 1))
    x = pick(own_ref, par_ref)
    mu, r, xhat = norm_stats(x)
    low = (xhat * vec(gain_ref, 0) + vec(shift_ref, 0)).astype(BF16)
    low_ref[...] = low
    logit = jnp.sum(x * center_ref[...].astype(F32), axis=1, keepdims=True)
    gate = jax.nn.sigmoid(logit)
    live = jnp.where(x[:, :1] < PAD_LIMIT, 1.0, 0.0)
    lane = lax.broadcasted_iota(jnp.int32, row_ref.shape, 1)
    row_ref[...] = jnp.where(lane == 0, mu, jnp.where(lane == 1, r, jnp.where(lane == 2, gate, live)))
    part = feed_forward(0, low, weights, b_in_ref, act_ref, slope_ref)
    part_ref[...] = part.astype(BF16)


def branch_kernel(part_ref, theirs_ref, row_ref, out_ref, branch_ref):
    out = part_ref[...] + theirs_ref[...].astype(F32)
    out_ref[...] = out.astype(BF16)
    branch_ref[...] = (row_ref[:, 2:3] * out).astype(BF16)


def start_sums(sums_ref):
    @pl.when(pl.program_id(0) == 0)
    def _():
        sums_ref[...] = jnp.zeros_like(sums_ref)


def back_feed(ds, weights, slope_ref, dh_ref, sums_ref):
    depth = ds.shape[1]
    dact = dot_nt(ds, weights.take(1))
    dh = (dact * slope_ref[...].astype(F32)).astype(BF16)
    dh_ref[...] = dh
    bias = row_sum(dh.astype(F32))
    for j in range(bias.shape[1] // depth):
        sums_ref[3 + j : 4 + j] += bias[:, j * depth : (j + 1) * depth]
    return dot_nt(dh, weights.take(0))


def second_kernel(
    x_own_ref, x_par_ref, mine_ref, theirs_ref, dy_own_ref, dy_par_ref, gate_ref,
    b_out_ref, gain_ref, shift_ref, b_in_ref, w_in_ref, w_out_ref,
    part_own_ref, part_par_ref, xhat_ref, row_ref, back_ref, low_ref, later_ref, sums_ref, grad_in_ref, grad_out_ref,
    w_in_buf, w_out_buf, sems, act_ref, slope_ref, ds_ref, dh_ref, sum_in_ref, sum_out_ref, out_sems,
):
    weights = Weights(1, (w_in_ref, w_out_ref, w_in_buf, w_out_buf, sems), (0, 1))
    start_sums(sums_ref)
    start_sums(sum_in_ref)
    start_sums(sum_out_ref)
    own = in_own_half()
    last = pl.program_id(0) == pl.num_programs(0) - 1
    half, depth = sum_out_ref.shape
    now = sum_in_ref.shape[1]
    h = pick(x_own_ref, x_par_ref) + vec(b_out_ref, 0) + (mine_ref[...].astype(F32) + theirs_ref[...].astype(F32))
    mu, r, xhat = norm_stats(h)
    low_ref[...] = (xhat * vec(gain_ref, 1) + vec(shift_ref, 1)).astype(BF16)
    xhat_ref[...] = xhat.astype(BF16)
    row_ref[...] = jnp.broadcast_to(r, row_ref.shape)
    ds = gate_ref[:, 2:3] * pick(dy_own_ref, dy_par_ref)
    ds_ref[...] = ds.astype(BF16)

    @pl.when(own)
    def _():
        part_own_ref[...] = h + vec(b_out_ref, 1)

    part = feed_forward(1, low_ref[...], weights, b_in_ref, act_ref, slope_ref)

    @pl.when(own)
    def _():
        part_own_ref[...] += part

    @pl.when(jnp.logical_not(own))
    def _():
        part_par_ref[...] = part.astype(BF16)

    sum_out_ref[...] += dot_tn(act_ref[...], ds_ref[...])
    out_copy = pltpu.make_async_copy(sum_out_ref, grad_out_ref.at[1, 0], out_sems.at[0])
    pl.when(last)(out_copy.start)
    dact = dot_nt(ds_ref[...], w_out_buf[...])
    dh_ref[...] = (dact * slope_ref[...].astype(F32)).astype(BF16)
    bias = row_sum(dh_ref[...].astype(F32))
    for j in range(half // depth):
        sums_ref[3 + j : 4 + j] += bias[:, j * depth : (j + 1) * depth]
    sum_in_ref[...] += dot_tn(low_ref[...], dh_ref[:, :now])
    later_ref[...] = dh_ref[:, now:]
    in_copy = pltpu.make_async_copy(sum_in_ref, grad_in_ref.at[1, 0, :, pl.ds(0, now)], out_sems.at[1])
    pl.when(last)(in_copy.start)
    dn = dot_nt(dh_ref[...], w_in_buf[...])
    back_ref[...] = dn.astype(BF16)
    sums_ref[0:1] += row_sum(dn * xhat)
    sums_ref[1:2] += row_sum(dn)
    sums_ref[2:3] += row_sum(ds_ref[...].astype(F32))

    @pl.when(last)
    def _():
        out_copy.wait()
        in_copy.wait()


def norm_back(dn, gain, xhat, r):
    dxhat = dn * gain
    m1 = jnp.mean(dxhat, axis=1, keepdims=True)
    m2 = jnp.mean(dxhat * xhat, axis=1, keepdims=True)
    return r * (dxhat - m1 - xhat * m2)


def back_first_kernel(
    own_ref, par_ref, row_ref, mine_ref, theirs_ref, xhat_ref, row1_ref, gain_ref, x_own_ref, x_par_ref, slope_ref,
    w_in_ref, w_out_ref, ds_ref, dh_ref, part_own_ref, carry_ref, part_par_ref, sums_ref, *bufs,
):
    weights = Weights(0, (w_in_ref, w_out_ref, *bufs), (1, 0))
    start_sums(sums_ref)
    own = in_own_half()
    dn = mine_ref[...].astype(F32) + theirs_ref[...].astype(F32)
    carry = row_ref[:, 2:3] * pick(own_ref, par_ref) + norm_back(
        dn, vec(gain_ref, 1), xhat_ref[...].astype(F32), row1_ref[:, 0:1]
    )
    ds = carry.astype(BF16)
    ds_ref[...] = ds

    @pl.when(own)
    def _():
        carry_ref[...] = carry

    dn = back_feed(ds, weights, slope_ref, dh_ref, sums_ref)
    xhat = (pick(x_own_ref, x_par_ref) - row_ref[:, 0:1]) * row_ref[:, 1:2]
    sums_ref[0:1] += row_sum(dn * xhat)
    sums_ref[1:2] += row_sum(dn)
    sums_ref[2:3] += row_sum(ds.astype(F32))

    @pl.when(own)
    def _():
        part_own_ref[...] = dn.astype(BF16)

    @pl.when(jnp.logical_not(own))
    def _():
        part_par_ref[...] = dn.astype(BF16)


def input_kernel(
    dy_ref, out_ref, row_ref, x_ref, part_ref, theirs_ref, carry_ref, gain_ref, center_ref, s0_ref, s1_ref,
    drow_ref, local_ref,
):
    @pl.when(pl.program_id(0) == 0)
    def _():
        local_ref[0:8] = s0_ref[...]
        local_ref[8:16] = s1_ref[...]
        local_ref[16:24] = jnp.zeros_like(local_ref[16:24])

    x = x_ref[...].astype(F32)
    gate = row_ref[:, 2:3]
    live = row_ref[:, 3:4]
    dgate = jnp.sum(dy_ref[...].astype(F32) * out_ref[...].astype(F32), axis=1, keepdims=True)
    dlogit = dgate * gate * (1.0 - gate)
    dn = part_ref[...].astype(F32) + theirs_ref[...].astype(F32)
    r = row_ref[:, 1:2]
    carry = carry_ref[...] + norm_back(dn, vec(gain_ref, 0), (x - row_ref[:, 0:1]) * r, r)
    drow_ref[...] = (carry + dlogit * center_ref[...].astype(F32)).astype(BF16)
    local_ref[16:17] += row_sum(dlogit * x)
    local_ref[17:18] += jnp.broadcast_to(row_sum(gate * live), (1, x.shape[1]))
    local_ref[18:19] += jnp.broadcast_to(row_sum(live), (1, x.shape[1]))


def finish_kernel(
    mean_load, here_ref, local_ref, other_ref, b_in_ref, b_out_ref, gain_ref, shift_ref, center_ref, gate_ref, load_ref
):
    depth = local_ref.shape[1]
    for layer in range(2):
        base = 8 * layer
        gain_ref[layer] = local_ref[base : base + 1] + other_ref[base : base + 1]
        shift_ref[layer] = local_ref[base + 1 : base + 2] + other_ref[base + 1 : base + 2]
        b_out_ref[layer] = local_ref[base + 2 : base + 3]
        parts = b_in_ref.shape[2] // (2 * depth)
        for side in range(2):

            @pl.when(here_ref[0] == side)
            def _():
                for j in range(parts):
                    low = (side * parts + j) * depth
                    b_in_ref[layer, :, low : low + depth] = local_ref[base + 3 + j : base + 4 + j]
                    low = ((1 - side) * parts + j) * depth
                    b_in_ref[layer, :, low : low + depth] = other_ref[base + 3 + j : base + 4 + j]

    total = local_ref[16:24] + other_ref[16:24]
    center_ref[...] = total[0:1]
    gate_ref[...] = total[1:2, :128] / total[2:3, :128]
    load_ref[...] = total[2:3, :128] / mean_load


def out_kernel(act_ref, ds_ref, _, out_ref):
    out_ref[...] = dot_tn(act_ref[...], ds_ref[...])


def out_gradient(act, ds, into, blk):
    rows, half = act.shape
    depth = ds.shape[1]
    return pl.pallas_call(
        out_kernel,
        grid=(half // blk,),
        in_specs=[
            pl.BlockSpec((rows, blk), lambda i: (0, i)),
            pl.BlockSpec((rows, depth), lambda i: (0, 0), pipeline_mode=pl.Buffered(1)),
            pl.BlockSpec(memory_space=pl.ANY),
        ],
        out_specs=pl.BlockSpec((None, None, blk, depth), lambda i: (0, 0, i, 0)),
        out_shape=sds(into.shape, F32),
        input_output_aliases={2: 0},
        compiler_params=params(),
        cost_estimate=cost(),
        name="out_gradient",
    )(to_hbm(act), to_hbm(ds), into)


def in_kernel(first, low0_ref, dh0_ref, low1_ref, dh1_ref, _, out_ref):
    step = pl.program_id(0)

    @pl.when(step < first)
    def _():
        out_ref[...] = dot_tn(low0_ref[...], dh0_ref[...])

    @pl.when(step >= first)
    def _():
        out_ref[...] = dot_tn(low1_ref[...], dh1_ref[...])


def in_gradient(low0, dh0, low1, dh1, into, blk):
    rows, half = dh0.shape
    depth = low0.shape[1]
    first, steps = half // blk, (half + dh1.shape[1]) // blk
    skip = first - dh1.shape[1] // blk
    fixed = pl.BlockSpec((rows, depth), lambda i: (0, 0), pipeline_mode=pl.Buffered(1))
    return pl.pallas_call(
        lambda *refs: in_kernel(first, *refs),
        grid=(steps,),
        in_specs=[
            fixed,
            pl.BlockSpec((rows, blk), lambda i: (0, jnp.minimum(i, first - 1))),
            fixed,
            pl.BlockSpec((rows, blk), lambda i: (0, jnp.maximum(i - first, 0))),
            pl.BlockSpec(memory_space=pl.ANY),
        ],
        out_specs=pl.BlockSpec(
            (None, None, depth, blk),
            lambda i: (i // first, 0, 0, jnp.where(i < first, i, i - first + skip)),
        ),
        out_shape=sds(into.shape, F32),
        input_output_aliases={4: 0},
        compiler_params=params(),
        cost_estimate=cost(),
        name="in_gradient",
    )(*(to_hbm(v) for v in (low0, dh0, low1, dh1)), into)


def on_device(tokens, routes, cotangent, ln_gain, ln_shift, w_in, b_in, w_out, b_out, centroid):
    experts = lax.axis_size("expert")
    replicas = lax.axis_size("replica")
    here = lax.axis_index("replica")
    tok_dev, depth = tokens.shape
    half = w_in.shape[3]
    capacity = 2 * tok_dev // experts
    slots = experts * capacity
    both = 2 * slots
    gain, shift, b_out = (v.reshape(2, depth) for v in (ln_gain, ln_shift, b_out))

    def exchange(v):
        moved = lax.all_to_all(
            v.reshape(experts, capacity, depth), "expert", split_axis=0, concat_axis=0, tiled=True
        )
        return moved.reshape(slots, depth)

    def swap(v):
        return lax.ppermute(v, "replica", SWAP)

    sent_tok, place = call(
        lambda *refs: pack_first_kernel(experts, capacity, *refs),
        "pack_first",
        (routes.reshape(1, tok_dev), tokens),
        [sds((slots, depth), BF16), sds((slots, tok_dev), BF16)],
    )
    b_half = lax.dynamic_slice_in_dim(b_in.reshape(2, 2 * half), here * half, half, axis=1)
    x_own = exchange(sent_tok)
    [sent_cot] = call(pack_kernel, "pack", (place, cotangent), [sds((slots, depth), BF16)])
    sent_cot, x_own = lax.optimization_barrier((sent_cot, x_own))
    x_par = swap(x_own)
    dy_own = exchange(sent_cot)

    narrow, wide = ("r", sds((both, depth), BF16)), ("r", sds((both, half), BF16))
    per_row = ("r", sds((both, 128), F32))
    own_sum, par_sum = ("o", sds((slots, depth), F32)), ("p", sds((slots, depth), BF16))
    sums = ("w", sds((8, depth), F32))
    x = (("o", x_own), ("p", x_par))
    low0, act0, slope0, p0, row = row_call(
        first_kernel,
        "forward_first",
        both,
        (*x, ("w", gain), ("w", shift), ("w", centroid), ("w", b_half)),
        [narrow, wide, wide, narrow, per_row],
        weights=(w_in, w_out),
        tile=256,
    )
    dy = (("o", dy_own), ("p", swap(dy_own)))
    p1_own, p1_par, xhat1, row1, n1, low1, dh1, sums1, grad_in, grad_out = row_call(
        second_kernel,
        "second",
        both,
        (
            *x, ("r", p0), ("s", swap(p0)), *dy, ("r", row),
            ("w", b_out), ("w", gain), ("w", shift), ("w", b_half),
        ),
        [own_sum, par_sum, narrow, per_row, narrow, narrow, ("r", sds((both, half // 4), BF16)), sums],
        sums=1,
        weights=(w_in, w_out),
        mib=46,
        far=(sds((2, 1, depth, half), F32), sds((2, 1, half, depth), F32)),
        scratch=[
            pltpu.VMEM((256, half), BF16),
            pltpu.VMEM((256, half), BF16),
            pltpu.VMEM((256, depth), BF16),
            pltpu.VMEM((256, half), BF16),
            pltpu.VMEM((depth, 3 * half // 4), F32),
            pltpu.VMEM((half, depth), F32),
            pltpu.SemaphoreType.DMA((2,)),
        ],
    )
    p1_there, n1 = lax.optimization_barrier((swap(p1_par), n1))
    out, branch = row_call(
        branch_kernel,
        "branch",
        slots,
        (("r", p1_own), ("r", p1_there), ("r", row)),
        [("r", sds((slots, depth), BF16))] * 2,
        mib=24,
    )
    returned = exchange(branch)
    ds0, dh0, n0_own, carry_own, n0_par, sums0 = row_call(
        back_first_kernel,
        "backward_first",
        both,
        (
            *dy, ("r", row), ("r", n1), ("s", swap(n1)), ("r", xhat1), ("r", row1), ("w", gain), *x, ("r", slope0),
        ),
        [narrow, wide, ("o", sds((slots, depth), BF16)), own_sum, par_sum, sums],
        sums=1,
        tile=256,
        weights=(w_in, w_out),
    )
    drow, local = row_call(
        input_kernel,
        "input_gradient",
        slots,
        (
            ("r", dy_own), ("r", out), ("r", row), ("r", x_own), ("r", n0_own), ("r", swap(n0_par)), ("r", carry_own),
            ("w", gain), ("w", centroid), ("w", sums0), ("w", sums1),
        ),
        [("r", sds((slots, depth), BF16)), ("w", sds((24, depth), F32))],
        sums=1,
        mib=24,
    )
    drow, returned = lax.optimization_barrier((drow, returned))
    grad_returned = exchange(drow)

    grad_out = out_gradient(act0, ds0, grad_out, 512)
    grad_in = in_gradient(low0, dh0, low1, dh1, grad_in, 512)
    [mixed] = call(unpack_kernel, "unpack", (place, returned, tokens), [sds(tokens.shape, BF16)])
    other = swap(local)
    one = sds((2, 1, depth), F32)
    grad_b_in, grad_b_out, grad_gain, grad_shift, grad_center, mean_gate, load = call(
        lambda *refs: finish_kernel(float(tok_dev * replicas), *refs),
        "finish",
        (here.astype(jnp.int32).reshape(1), local, other),
        [sds((2, 1, 2 * half), F32), one, one, one, sds((1, depth), F32), sds((1, 128), F32), sds((1, 128), F32)],
        smem_in=1,
    )
    [grad_tokens] = call(unpack_kernel, "unpack", (place, grad_returned, cotangent), [sds(tokens.shape, BF16)])
    return (
        mixed, grad_tokens, grad_in, grad_out, grad_b_in, grad_b_out, grad_gain, grad_shift, grad_center,
        mean_gate[0, :1], load[0, :1],
    )


def solution(mesh):
    rows = P(("expert", "replica"), None)
    by_expert = P(None, "expert", None)
    first_weight = P(None, "expert", None, "replica")
    second_weight = P(None, "expert", "replica", None)
    return jax.shard_map(
        on_device,
        mesh=mesh,
        in_specs=(
            rows, rows, rows, by_expert, by_expert, first_weight, by_expert, second_weight, by_expert,
            P("expert", None),
        ),
        out_specs=(
            rows, rows, first_weight, second_weight, by_expert, by_expert, by_expert, by_expert,
            P("expert", None), P("expert"), P("expert"),
        ),
        check_vma=False,
    )
```
